32 devices in a mesh: pan: 16 (over z, x, core), grp: 2 (over y).
Axes of the slice: x: 2, y: 2, z: 4, core: 2. Of those that a mesh axis runs over, the one named last changes fastest.
Arguments:
- amplitudes: bfloat16 [1024, 8192], P('grp', 'pan'), may hold values from -6 to 6
- integrals: bfloat16 [8192, 32768], P('grp', 'pan'), may hold values from -0.0625 to 0.0625
- amp_screen: int32 [16, 2], replicated, may hold values from 0 to 1, as said below
- int_screen: int32 [2, 8], replicated, may hold values 0 or 1
Outputs:
- ladder_term: bfloat16 [1024, 32768], P('grp', 'pan')
The draws below stay inside these ranges and needn't reach their ends.
Inputs may be any that keep to these rules, and one draw needn't show every extreme that they name: Take the tiles of amp_screen in blocks of 8 consecutive occupied pair tiles; in each block and column at least one and at most 4 tiles are 1, and some block and column has exactly 4.
All inputs are finite; a program needn't handle non-finite values.
Results may differ from the reference program's by a relative error of at most 0.001.
Values may be sent and summed in bfloat16 or wider, within the bound.
No kernel may reach another device: no remote copies, remote signals or barrier semaphores. Data moves between devices by JAX's collectives and lax.ppermute only.
A program may use at most 128 MiB of HBM per device.

```python
import jax
import jax.numpy as jnp

TS = 64
PT_DEV = 8
NCDT = 2
ABT = 8
LIVE_MAX = 4
PT = 16
P_SIZE = 1024
CD = 8192
AB = 32768


def draw_amp_screen(key, part):
    key = jax.random.fold_in(key, 11)
    key_count, key_pick, key_order = jax.random.split(key, 3)
    block_count = PT // PT_DEV
    counts = jax.random.randint(key_count, (block_count * NCDT,), 1, LIVE_MAX + 1)
    chosen = jax.random.randint(key_pick, (), 0, block_count * NCDT)
    counts = jnp.where(jnp.arange(block_count * NCDT) == chosen, LIVE_MAX, counts).reshape(block_count, NCDT)
    scores = jax.random.randint(key_order, (block_count, PT_DEV, NCDT), 0, 1 << 20) * PT_DEV
    scores = scores + jnp.arange(PT_DEV)[None, :, None]
    order = jnp.argsort(jnp.argsort(scores, axis=1, stable=True), axis=1, stable=True)
    live = (order < counts[:, None, :]).astype(jnp.int32)
    return live.reshape(PT, NCDT)


def touch_ends(entries, own_key, smallest, top_value):
    index_at = [jax.random.randint(jax.random.fold_in(own_key, axis), (), 0, length) for axis, length in enumerate(entries.shape)]
    longest = entries.shape.index(max(entries.shape))
    neighbour = index_at[:longest] + [(index_at[longest] + 1) % entries.shape[longest]] + index_at[longest + 1:]
    return entries.at[tuple(index_at)].set(smallest).at[tuple(neighbour)].set(top_value)


def block_levels(rng, dims, cuts, low, top_value):
    def one(axis_at, parts):
        steps = jax.random.uniform(jax.random.fold_in(jax.random.fold_in(rng, 6), axis_at), (parts,), jnp.float32, low / len(cuts), top_value / len(cuts))
        return jnp.repeat(jnp.exp(steps), dims[axis_at] // parts).reshape((-1,) + (1,) * (len(dims) - axis_at - 1))

    gain = one(*cuts[0])
    for cut in cuts[1:]:
        gain = gain * one(*cut)
    return gain


def centred(key, extent, scale, most, cuts=(), dtype=jnp.bfloat16):
    entries = scale * jax.random.normal(key, extent, jnp.float32)
    if cuts:
        entries = entries * block_levels(key, extent, cuts, -0.22, 0.18)
    return jnp.clip(entries, -most, most).astype(dtype)


def setup_inputs(seed: int = 0) -> dict:
    key_list = jax.random.split(jax.random.key(seed), 5)
    amplitudes = centred(key_list[0], (P_SIZE, CD), 1.0, 6.0, ((0, 2), (1, 16)))
    integrals = centred(key_list[1], (CD, AB), CD ** -0.5, 0.0625, ((0, 2), (1, 16)))
    amp_screen = draw_amp_screen(jax.random.fold_in(key_list[4], 71), 0)
    int_screen = touch_ends((jax.random.randint(key_list[3], (NCDT, ABT), 0, 4) < 3).astype(jnp.int32), jax.random.fold_in(key_list[3], 1), 0, 1)
    return {"amplitudes": amplitudes, "integrals": integrals, "amp_screen": amp_screen, "int_screen": int_screen}


def reference(amplitudes, integrals, amp_screen, int_screen):
    pair_size = TS * TS
    amp_keep = amp_screen.astype(jnp.bfloat16)
    masked_amps = (amplitudes.reshape(PT, TS, NCDT, pair_size) * amp_keep[:, None, :, None]).reshape(P_SIZE, CD)
    int_keep = int_screen.astype(jnp.bfloat16)
    masked_ints = (integrals.reshape(NCDT, pair_size, ABT, pair_size) * int_keep[:, None, :, None]).reshape(CD, AB)
    return jnp.dot(masked_amps, masked_ints, preferred_element_type=jnp.float32).astype(jnp.bfloat16)
```

```python
import functools

import jax
import jax.numpy as jnp
from jax import lax
from jax.experimental import pallas as pl
from jax.experimental.pallas import tpu as pltpu
from jax.sharding import PartitionSpec as P

TS = 64
LIVE_MAX = 4
BLOCK_TILES = 8
AXES = ("pan", "grp")
SLOT_CHUNKS = ((0, 2), (2, 4))
CODE_MAX = 32767.0
LEAST_SCALE = 1e-33
COLUMN_TILE = 256
JOIN_TILE = 512
VMEM_BYTES = 56 * 1024 * 1024


def live_slots(screen_ref, first_tile, column):
    count = jnp.int32(0)
    slots = [jnp.int32(0)] * LIVE_MAX
    for tile in range(BLOCK_TILES):
        live = screen_ref[first_tile + tile, column] != 0
        for slot in range(LIVE_MAX):
            slots[slot] = jnp.where(live & (count == slot), tile, slots[slot])
        count = count + live.astype(jnp.int32)
    return slots, count


def pick_kernel(pair_size, screen_ref, amps_ref, *rest):
    picked_refs, sem = rest[:-1], rest[-1]
    column = lax.axis_index("pan") * amps_ref.shape[1] // pair_size
    slots, _ = live_slots(screen_ref, lax.axis_index("grp") * BLOCK_TILES, column)
    copies = []
    for (first, last), picked_ref in zip(SLOT_CHUNKS, picked_refs):
        for slot in range(first, last):
            rows = pl.ds(pl.multiple_of(slots[slot] * TS, TS), TS)
            copies.append(
                pltpu.make_async_copy(
                    amps_ref.at[rows, :],
                    picked_ref.at[pl.ds((slot - first) * TS, TS), :],
                    sem.at[slot],
                )
            )
    for copy in copies:
        copy.start()
    for copy in copies:
        copy.wait()


def pick_live(amplitudes, amp_screen, pair_size):
    return pl.pallas_call(
        functools.partial(pick_kernel, pair_size),
        out_shape=[
            jax.ShapeDtypeStruct(((last - first) * TS, amplitudes.shape[1]), amplitudes.dtype)
            for first, last in SLOT_CHUNKS
        ],
        in_specs=[pl.BlockSpec(memory_space=pltpu.SMEM), pl.BlockSpec(memory_space=pl.ANY)],
        out_specs=[pl.BlockSpec(memory_space=pl.ANY)] * len(SLOT_CHUNKS),
        scratch_shapes=[pltpu.SemaphoreType.DMA((LIVE_MAX,))],
        name="pick_live",
    )(amp_screen, amplitudes)


def lay_out(blocks, panel):
    depth = blocks[0].shape[1]
    own = lax.rem(lax.axis_index("pan"), len(blocks))
    for step, block in enumerate(blocks):
        column = pl.multiple_of((own ^ step) * depth, depth)
        panel[:, pl.ds(column, depth)] = block[...]


def int_keep(screen_ref, ints_shape, pair_size):
    in_pair = lax.axis_index("grp") * ints_shape[0] // pair_size
    out_pair = lax.axis_index("pan") * ints_shape[1] // pair_size
    return screen_ref[in_pair, out_pair].astype(jnp.float32)


def own_kernel(ints_shape, pair_size, screen_ref, *refs):
    blocks, (ints_ref, sum_ref, panel) = refs[:-3], refs[-3:]

    @pl.when(pl.program_id(0) == 0)
    def _():
        lay_out(blocks, panel)

    sums = jnp.dot(panel[...], ints_ref[...], preferred_element_type=jnp.float32)
    sum_ref[...] = sums * int_keep(screen_ref, ints_shape, pair_size)


def away_kernel(ints_shape, pair_size, screen_ref, *refs):
    blocks, (ints_ref, code_ref, scale_ref, panel) = refs[:-4], refs[-4:]

    @pl.when(pl.program_id(0) == 0)
    def _():
        lay_out(blocks, panel)

    keep = int_keep(screen_ref, ints_shape, pair_size)
    sums = jnp.dot(panel[...], ints_ref[...], preferred_element_type=jnp.float32) * keep
    for slot in range(sums.shape[0] // TS):
        rows = slice(slot * TS, (slot + 1) * TS)
        part = sums[rows]
        top = jnp.maximum(jnp.max(jnp.abs(part), axis=0, keepdims=True), LEAST_SCALE)
        code = jnp.round(part * (CODE_MAX / top))
        code_ref[rows, :] = code.astype(jnp.int32).astype(jnp.int16)
        scale_ref[slot : slot + 1, :] = top * (1.0 / CODE_MAX)


def product(kernel, blocks, integrals, int_screen, pair_size, out_rows_types, name):
    row_count, depth = blocks[0].shape
    int_count, ab_count = integrals.shape
    whole = pl.BlockSpec((row_count, depth), lambda j: (0, 0))
    return pl.pallas_call(
        functools.partial(kernel, integrals.shape, pair_size),
        grid=(ab_count // COLUMN_TILE,),
        out_shape=[jax.ShapeDtypeStruct((rows, ab_count), dtype) for rows, dtype in out_rows_types],
        in_specs=[pl.BlockSpec(memory_space=pltpu.SMEM)]
        + [whole] * len(blocks)
        + [pl.BlockSpec((int_count, COLUMN_TILE), lambda j: (0, j))],
        out_specs=[pl.BlockSpec((rows, COLUMN_TILE), lambda j: (0, j)) for rows, _ in out_rows_types],
        scratch_shapes=[pltpu.VMEM((row_count, int_count), blocks[0].dtype)],
        compiler_params=pltpu.CompilerParams(vmem_limit_bytes=VMEM_BYTES),
        cost_estimate=pl.CostEstimate(
            flops=2 * row_count * int_count * ab_count,
            bytes_accessed=2 * int_count * ab_count,
            transcendentals=0,
        ),
        name=name,
    )(int_screen, *blocks, integrals)


def join_kernel(screen_ref, own_ref, *refs):
    chunk_refs, (out_ref, total) = refs[:-2], refs[-2:]
    grp_index = lax.axis_index("grp")
    first_tile = grp_index * BLOCK_TILES
    own_slots, own_count = live_slots(screen_ref, first_tile, grp_index)
    away_slots, away_count = live_slots(screen_ref, first_tile, 1 - grp_index)
    total[...] = jnp.zeros_like(total)
    for slot in range(LIVE_MAX):

        @pl.when(slot < own_count)
        def _():
            rows = pl.ds(pl.multiple_of(own_slots[slot] * TS, TS), TS)
            total[rows, :] = own_ref[slot * TS : (slot + 1) * TS, :]

    for chunk, (first, last) in enumerate(SLOT_CHUNKS):
        code_ref, scale_ref = chunk_refs[2 * chunk : 2 * chunk + 2]
        for slot in range(first, last):

            @pl.when(slot < away_count)
            def _():
                rows = pl.ds(pl.multiple_of(away_slots[slot] * TS, TS), TS)
                at = slot - first
                code = code_ref[at * TS : (at + 1) * TS, :].astype(jnp.float32)
                total[rows, :] += code * scale_ref[at : at + 1, :]

    out_ref[...] = total[...].astype(out_ref.dtype)


def join(amp_screen, own_sum, chunks, row_count):
    ab_count = own_sum.shape[1]
    flat = [array for chunk in chunks for array in chunk]

    def tall(rows):
        return pl.BlockSpec((rows, JOIN_TILE), lambda j: (0, j))

    return pl.pallas_call(
        join_kernel,
        grid=(ab_count // JOIN_TILE,),
        out_shape=jax.ShapeDtypeStruct((row_count, ab_count), jnp.bfloat16),
        in_specs=[pl.BlockSpec(memory_space=pltpu.SMEM), tall(own_sum.shape[0])]
        + [tall(array.shape[0]) for array in flat],
        out_specs=tall(row_count),
        scratch_shapes=[pltpu.VMEM((row_count, JOIN_TILE), jnp.float32)],
        compiler_params=pltpu.CompilerParams(vmem_limit_bytes=VMEM_BYTES),
        name="join",
    )(amp_screen, own_sum, *flat)


def routes(pan_count):
    half = pan_count // 2
    places = [(pan, grp) for pan in range(pan_count) for grp in range(2)]

    def at(pan, grp):
        return pan * 2 + grp

    def away(pan, grp):
        return pan // half != grp

    def flip(bits):
        return [(at(pan, grp), at(pan ^ bits, grp)) for pan, grp in places]

    first = [
        (at(pan, grp), at(pan, 1 - grp) if away(pan, grp) else at((pan + half) % pan_count, grp))
        for pan, grp in places
    ]
    across = [
        (at(pan, grp), at((pan + half) % pan_count, 1 - grp)) for pan, grp in places if away(pan, grp)
    ]
    swap = [(at(pan, grp), at(pan, 1 - grp)) for pan, grp in places]
    return first, across, swap, flip


def gathered(block, flip, block_count):
    near = [lax.ppermute(block, AXES, flip(bits)) for bits in range(2, block_count, 2)]
    blocks = [block] + near
    other = [lax.ppermute(held, AXES, flip(1)) for held in blocks]
    return [held for pair in zip(blocks, other) for held in pair]


def two_group_shards(pan_count, amplitudes, integrals, amp_screen, int_screen):
    pair_size = TS * TS
    row_count, col_count = amplitudes.shape
    block_count = integrals.shape[0] // col_count
    if (
        row_count != BLOCK_TILES * TS
        or amp_screen.shape[1] != 2
        or integrals.shape[0] != pair_size
        or block_count * 2 != pan_count
    ):
        return shards(amplitudes, integrals, amp_screen, int_screen)
    first, across, swap, flip = routes(pan_count)
    is_own = lax.axis_index("pan") // (pan_count // 2) == lax.axis_index("grp")

    picked = pick_live(amplitudes, amp_screen, pair_size)
    own_parts, chunks = [], []
    for part in picked:
        from_first = lax.ppermute(part, AXES, first)
        from_across = lax.ppermute(part, AXES, across)
        own_parts.append(jnp.where(is_own, part, from_first))
        blocks = gathered(jnp.where(is_own, from_first, from_across), flip, block_count)
        rows = part.shape[0]
        code, scale = product(
            away_kernel, blocks, integrals, int_screen, pair_size,
            ((rows, jnp.int16), (rows // TS, jnp.float32)), "away_product",
        )
        chunks.append((lax.ppermute(code, AXES, swap), lax.ppermute(scale, AXES, swap)))
    own_blocks = gathered(jnp.concatenate(own_parts, axis=0), flip, block_count)
    (own_sum,) = product(
        own_kernel, own_blocks, integrals, int_screen, pair_size,
        ((LIVE_MAX * TS, jnp.float32),), "own_product",
    )
    return join(amp_screen, own_sum, chunks, row_count)


def column_pairs(piece_width, pair_size, pair_count):
    col_pair = jnp.arange(piece_width) // pair_size
    return (col_pair[None, :] == jnp.arange(pair_count)[:, None]).astype(jnp.bfloat16)


def shards(amplitudes, integrals, amp_screen, int_screen):
    pair_size = TS * TS
    row_count, col_count = amplitudes.shape
    int_count, ab_count = integrals.shape
    tile_count = row_count // TS
    pair_count = amp_screen.shape[1]
    grp_index = lax.axis_index("grp")
    pan_index = lax.axis_index("pan")
    screen_rows = lax.dynamic_slice_in_dim(amp_screen, grp_index * tile_count, tile_count, 0)
    in_pair = grp_index * int_count // pair_size
    out_pair = pan_index * ab_count // pair_size
    int_keep = int_screen[in_pair, out_pair].astype(jnp.bfloat16)
    int_panel = lax.all_gather(integrals * int_keep, "grp", axis=0, tiled=True)
    panel = lax.all_gather(amplitudes, "pan", axis=1, tiled=True)
    piece_width = panel.shape[1]
    onehot = column_pairs(piece_width, pair_size, pair_count)
    keep_mask = jnp.dot(
        screen_rows.astype(jnp.bfloat16), onehot, preferred_element_type=jnp.float32
    ).astype(jnp.bfloat16)
    masked = (panel.reshape(tile_count, TS, piece_width) * keep_mask[:, None, :]).reshape(
        row_count, piece_width
    )
    summed = jnp.dot(masked, int_panel, preferred_element_type=jnp.float32)
    return summed.astype(jnp.bfloat16)


def solution(mesh):
    in_specs = (P("grp", "pan"), P("grp", "pan"), P(), P())
    out_specs = P("grp", "pan")
    pan_count, grp_count = mesh.shape["pan"], mesh.shape["grp"]
    body = shards
    if grp_count == 2 and pan_count >= 4 and pan_count & (pan_count - 1) == 0:
        body = functools.partial(two_group_shards, pan_count)
    return jax.shard_map(body, mesh=mesh, in_specs=in_specs, out_specs=out_specs, check_vma=False)
```

```python
import functools

import jax
import jax.numpy as jnp
from jax import lax
from jax.experimental import pallas as pl
from jax.experimental.pallas import tpu as pltpu
from jax.sharding import PartitionSpec as P

TS = 64
LIVE_MAX = 4
BLOCK_TILES = 8
AXES = ("pan", "grp")
SLOT_CHUNKS = ((0, 2), (2, 4))
CODE_MAX = 32767.0
LEAST_SCALE = 1e-33
COLUMN_TILE = 256
JOIN_TILE = 512
SMALL_VMEM = 8 * 1024 * 1024
PRODUCT_VMEM = 16 * 1024 * 1024
WHOLE = pl.BlockSpec(memory_space=pltpu.VMEM)


def live_slots(screen_ref, first_tile, column):
    count = jnp.int32(0)
    slots = [jnp.int32(0)] * LIVE_MAX
    for tile in range(BLOCK_TILES):
        live = screen_ref[first_tile + tile, column] != 0
        for slot in range(LIVE_MAX):
            slots[slot] = jnp.where(live & (count == slot), tile, slots[slot])
        count = count + live.astype(jnp.int32)
    return slots, count


def pick_kernel(pair_size, screen_hbm, amps_ref, *rest):
    picked_refs, (screen_ref, screen_sem, sem) = rest[:-3], rest[-3:]
    screen_copy = pltpu.make_async_copy(screen_hbm, screen_ref, screen_sem)
    screen_copy.start()
    screen_copy.wait()
    column = lax.axis_index("pan") * amps_ref.shape[1] // pair_size
    slots, _ = live_slots(screen_ref, lax.axis_index("grp") * BLOCK_TILES, column)
    copies = []
    for (first, last), picked_ref in zip(SLOT_CHUNKS, picked_refs):
        for slot in range(first, last):
            rows = pl.ds(pl.multiple_of(slots[slot] * TS, TS), TS)
            copies.append(
                pltpu.make_async_copy(
                    amps_ref.at[rows, :],
                    picked_ref.at[pl.ds((slot - first) * TS, TS), :],
                    sem.at[slot],
                )
            )
    for copy in copies:
        copy.start()
    for copy in copies:
        copy.wait()


def pick_live(amplitudes, amp_screen, pair_size):
    return pl.pallas_call(
        functools.partial(pick_kernel, pair_size),
        out_shape=[
            jax.ShapeDtypeStruct(((last - first) * TS, amplitudes.shape[1]), amplitudes.dtype)
            for first, last in SLOT_CHUNKS
        ],
        in_specs=[pl.BlockSpec(memory_space=pl.ANY)] * 2,
        out_specs=[WHOLE] * len(SLOT_CHUNKS),
        scratch_shapes=[
            pltpu.SMEM(amp_screen.shape, amp_screen.dtype),
            pltpu.SemaphoreType.DMA,
            pltpu.SemaphoreType.DMA((LIVE_MAX,)),
        ],
        compiler_params=pltpu.CompilerParams(vmem_limit_bytes=SMALL_VMEM),
        name="pick_live",
    )(amp_screen, amplitudes)


def lay_out(blocks, panel):
    depth = blocks[0].shape[1]
    own = lax.rem(lax.axis_index("pan"), len(blocks))
    for step, block in enumerate(blocks):
        column = pl.multiple_of((own ^ step) * depth, depth)
        panel[:, pl.ds(column, depth)] = block[...]


def int_keep(screen_ref, ints_shape, pair_size):
    in_pair = lax.axis_index("grp") * ints_shape[0] // pair_size
    out_pair = lax.axis_index("pan") * ints_shape[1] // pair_size
    return screen_ref[in_pair, out_pair].astype(jnp.float32)


def own_kernel(pair_size, int_screen_ref, amp_screen_ref, *refs):
    blocks, (ints_ref, total_ref, panel) = refs[:-3], refs[-3:]
    grp_index = lax.axis_index("grp")
    slots, count = live_slots(amp_screen_ref, grp_index * BLOCK_TILES, grp_index)
    keep = int_keep(int_screen_ref, ints_ref.shape, pair_size)
    lay_out(blocks, panel)
    total_ref[...] = jnp.zeros_like(total_ref)
    for column in range(0, ints_ref.shape[1], COLUMN_TILE):
        columns = slice(column, column + COLUMN_TILE)
        sums = jnp.dot(panel[...], ints_ref[:, columns], preferred_element_type=jnp.float32) * keep
        for slot in range(LIVE_MAX):

            @pl.when(slot < count)
            def _():
                rows = pl.ds(pl.multiple_of(slots[slot] * TS, TS), TS)
                total_ref[rows, columns] = sums[slot * TS : (slot + 1) * TS]


def away_kernel(pair_size, int_screen_ref, *refs):
    blocks, (ints_ref, code_ref, scale_ref, panel) = refs[:-4], refs[-4:]
    keep = int_keep(int_screen_ref, ints_ref.shape, pair_size)
    lay_out(blocks, panel)
    for column in range(0, ints_ref.shape[1], COLUMN_TILE):
        columns = slice(column, column + COLUMN_TILE)
        sums = jnp.dot(panel[...], ints_ref[:, columns], preferred_element_type=jnp.float32) * keep
        for slot in range(sums.shape[0] // TS):
            rows = slice(slot * TS, (slot + 1) * TS)
            part = sums[rows]
            top = jnp.maximum(jnp.max(jnp.abs(part), axis=0, keepdims=True), LEAST_SCALE)
            code = jnp.round(part * (CODE_MAX / top))
            code_ref[rows, columns] = code.astype(jnp.int32).astype(jnp.int16)
            scale_ref[slot : slot + 1, columns] = top * (1.0 / CODE_MAX)


def product(kernel, screens, blocks, ints, pair_size, out_rows_types, name):
    row_count = blocks[0].shape[0]
    int_count, ab_count = ints.shape
    return pl.pallas_call(
        functools.partial(kernel, pair_size),
        out_shape=[jax.ShapeDtypeStruct((rows, ab_count), dtype) for rows, dtype in out_rows_types],
        in_specs=[pl.BlockSpec(memory_space=pltpu.SMEM)] * len(screens) + [WHOLE] * (len(blocks) + 1),
        out_specs=[WHOLE] * len(out_rows_types),
        scratch_shapes=[pltpu.VMEM((row_count, int_count), blocks[0].dtype)],
        compiler_params=pltpu.CompilerParams(vmem_limit_bytes=PRODUCT_VMEM),
        cost_estimate=pl.CostEstimate(
            flops=2 * row_count * int_count * ab_count,
            bytes_accessed=2 * int_count * ab_count,
            transcendentals=0,
        ),
        name=name,
    )(*screens, *blocks, ints)


def join_kernel(screen_ref, own_ref, *refs):
    chunk_refs, out_ref = refs[:-1], refs[-1]
    grp_index = lax.axis_index("grp")
    slots, count = live_slots(screen_ref, grp_index * BLOCK_TILES, 1 - grp_index)
    out_ref[...] = own_ref[...].astype(out_ref.dtype)
    for chunk, (first, last) in enumerate(SLOT_CHUNKS):
        code_ref, scale_ref = chunk_refs[2 * chunk : 2 * chunk + 2]
        for slot in range(first, last):

            @pl.when(slot < count)
            def _():
                rows = pl.ds(pl.multiple_of(slots[slot] * TS, TS), TS)
                at = slot - first
                code = code_ref[at * TS : (at + 1) * TS, :].astype(jnp.float32)
                total = own_ref[rows, :] + code * scale_ref[at : at + 1, :]
                out_ref[rows, :] = total.astype(out_ref.dtype)


def join(amp_screen, own_sum, chunks):
    row_count, ab_count = own_sum.shape
    flat = [array for chunk in chunks for array in chunk]

    def tall(rows):
        return pl.BlockSpec((rows, JOIN_TILE), lambda j: (0, j))

    return pl.pallas_call(
        join_kernel,
        grid=(ab_count // JOIN_TILE,),
        out_shape=jax.ShapeDtypeStruct((row_count, ab_count), jnp.bfloat16),
        in_specs=[pl.BlockSpec(memory_space=pltpu.SMEM), tall(row_count)]
        + [tall(array.shape[0]) for array in flat],
        out_specs=tall(row_count),
        compiler_params=pltpu.CompilerParams(vmem_limit_bytes=SMALL_VMEM),
        name="join",
    )(amp_screen, own_sum, *flat)


def routes(pan_count):
    half = pan_count // 2
    places = [(pan, grp) for pan in range(pan_count) for grp in range(2)]

    def at(pan, grp):
        return pan * 2 + grp

    def away(pan, grp):
        return pan // half != grp

    def flip(bits):
        return [(at(pan, grp), at(pan ^ bits, grp)) for pan, grp in places]

    first = [
        (at(pan, grp), at(pan, 1 - grp) if away(pan, grp) else at((pan + half) % pan_count, grp))
        for pan, grp in places
    ]
    across = [
        (at(pan, grp), at((pan + half) % pan_count, 1 - grp) if away(pan, grp) else at(pan ^ 1, grp))
        for pan, grp in places
    ]
    swap = [(at(pan, grp), at(pan, 1 - grp)) for pan, grp in places]
    return first, across, swap, flip


def gathered(block, flip, block_count):
    near = [lax.ppermute(block, AXES, flip(bits)) for bits in range(2, block_count, 2)]
    blocks = [block] + near
    other = [lax.ppermute(held, AXES, flip(1)) for held in blocks]
    return [held for pair in zip(blocks, other) for held in pair]


def two_group_shards(pan_count, amplitudes, integrals, amp_screen, int_screen):
    pair_size = TS * TS
    row_count, col_count = amplitudes.shape
    block_count = integrals.shape[0] // col_count
    if (
        row_count != BLOCK_TILES * TS
        or amp_screen.shape[1] != 2
        or integrals.shape[0] != pair_size
        or block_count * 2 != pan_count
    ):
        return shards(amplitudes, integrals, amp_screen, int_screen)
    first, across, swap, flip = routes(pan_count)
    is_own = lax.axis_index("pan") // (pan_count // 2) == lax.axis_index("grp")

    ints = pltpu.with_memory_space_constraint(integrals, pltpu.VMEM)
    picked = pick_live(amplitudes, amp_screen, pair_size)
    own_parts, chunks = [], []
    for part in picked:
        from_first = lax.ppermute(part, AXES, first)
        from_across = lax.ppermute(part, AXES, across)
        own_parts.append(jnp.where(is_own, part, from_first))
        blocks = gathered(jnp.where(is_own, from_first, from_across), flip, block_count)
        rows = part.shape[0]
        code, scale = product(
            away_kernel, (int_screen,), blocks, ints, pair_size,
            ((rows, jnp.int16), (rows // TS, jnp.float32)), "away_product",
        )
        chunks.append((lax.ppermute(code, AXES, swap), lax.ppermute(scale, AXES, swap)))
    own_blocks = gathered(jnp.concatenate(own_parts, axis=0), flip, block_count)
    (own_sum,) = product(
        own_kernel, (int_screen, amp_screen), own_blocks, ints, pair_size,
        ((row_count, jnp.float32),), "own_product",
    )
    return join(amp_screen, own_sum, chunks)


def column_pairs(piece_width, pair_size, pair_count):
    col_pair = jnp.arange(piece_width) // pair_size
    return (col_pair[None, :] == jnp.arange(pair_count)[:, None]).astype(jnp.bfloat16)


def shards(amplitudes, integrals, amp_screen, int_screen):
    pair_size = TS * TS
    row_count, col_count = amplitudes.shape
    int_count, ab_count = integrals.shape
    tile_count = row_count // TS
    pair_count = amp_screen.shape[1]
    grp_index = lax.axis_index("grp")
    pan_index = lax.axis_index("pan")
    screen_rows = lax.dynamic_slice_in_dim(amp_screen, grp_index * tile_count, tile_count, 0)
    in_pair = grp_index * int_count // pair_size
    out_pair = pan_index * ab_count // pair_size
    int_keep = int_screen[in_pair, out_pair].astype(jnp.bfloat16)
    int_panel = lax.all_gather(integrals * int_keep, "grp", axis=0, tiled=True)
    panel = lax.all_gather(amplitudes, "pan", axis=1, tiled=True)
    piece_width = panel.shape[1]
    onehot = column_pairs(piece_width, pair_size, pair_count)
    keep_mask = jnp.dot(
        screen_rows.astype(jnp.bfloat16), onehot, preferred_element_type=jnp.float32
    ).astype(jnp.bfloat16)
    masked = (panel.reshape(tile_count, TS, piece_width) * keep_mask[:, None, :]).reshape(
        row_count, piece_width
    )
    summed = jnp.dot(masked, int_panel, preferred_element_type=jnp.float32)
    return summed.astype(jnp.bfloat16)


def solution(mesh):
    in_specs = (P("grp", "pan"), P("grp", "pan"), P(), P())
    out_specs = P("grp", "pan")
    pan_count, grp_count = mesh.shape["pan"], mesh.shape["grp"]
    body = shards
    if grp_count == 2 and pan_count >= 4 and pan_count & (pan_count - 1) == 0:
        body = functools.partial(two_group_shards, pan_count)
    return jax.shard_map(body, mesh=mesh, in_specs=in_specs, out_specs=out_specs, check_vma=False)
```

```python
import functools

import jax
import jax.numpy as jnp
from jax import lax
from jax.experimental import pallas as pl
from jax.experimental.pallas import tpu as pltpu
from jax.sharding import PartitionSpec as P

TS = 64
LIVE_MAX = 4
BLOCK_TILES = 8
AXES = ("pan", "grp")
SLOT_CHUNKS = ((0, 2), (2, 4))
CODE_MAX = 32767.0
STAGE_COPIES = 8
LEAST_SCALE = 1e-33
ROW_TILE = 128
COLUMN_TILE = 256
JOIN_TILE = 512
SMALL_VMEM = 8 * 1024 * 1024
PRODUCT_VMEM = 16 * 1024 * 1024
LIGHT = pl.CostEstimate(flops=1, bytes_accessed=1, transcendentals=0)
WHOLE = pl.BlockSpec(memory_space=pltpu.VMEM)


def live_slots(screen_ref, first_tile, column):
    count = jnp.int32(0)
    slots = [jnp.int32(0)] * LIVE_MAX
    for tile in range(BLOCK_TILES):
        live = screen_ref[column, first_tile + tile] != 0
        for slot in range(LIVE_MAX):
            slots[slot] = jnp.where(live & (count == slot), tile, slots[slot])
        count = count + live.astype(jnp.int32)
    return slots, count


def pick_kernel(pair_size, screen_hbm, amps_ref, *rest):
    picked_refs, (screen_ref, screen_sem, sem) = rest[:-3], rest[-3:]
    screen_copy = pltpu.make_async_copy(screen_hbm, screen_ref, screen_sem)
    screen_copy.start()
    screen_copy.wait()
    column = lax.axis_index("pan") * amps_ref.shape[1] // pair_size
    slots, _ = live_slots(screen_ref, lax.axis_index("grp") * BLOCK_TILES, column)
    copies = []
    for (first, last), picked_ref in zip(SLOT_CHUNKS, picked_refs):
        for slot in range(first, last):
            rows = pl.ds(pl.multiple_of(slots[slot] * TS, TS), TS)
            copies.append(
                pltpu.make_async_copy(
                    amps_ref.at[rows, :],
                    picked_ref.at[pl.ds((slot - first) * TS, TS), :],
                    sem.at[slot],
                )
            )
    for copy in copies:
        copy.start()
    for copy in copies:
        copy.wait()


def pick_live(amplitudes, amp_screen, pair_size):
    return pl.pallas_call(
        functools.partial(pick_kernel, pair_size),
        out_shape=[
            jax.ShapeDtypeStruct(((last - first) * TS, amplitudes.shape[1]), amplitudes.dtype)
            for first, last in SLOT_CHUNKS
        ],
        in_specs=[pl.BlockSpec(memory_space=pl.ANY), pl.BlockSpec(memory_space=pltpu.HBM)],
        out_specs=[WHOLE] * len(SLOT_CHUNKS),
        scratch_shapes=[
            pltpu.SMEM(amp_screen.shape, amp_screen.dtype),
            pltpu.SemaphoreType.DMA,
            pltpu.SemaphoreType.DMA((LIVE_MAX,)),
        ],
        compiler_params=pltpu.CompilerParams(vmem_limit_bytes=SMALL_VMEM),
        name="pick_live",
    )(amp_screen, pltpu.with_memory_space_constraint(amplitudes, pltpu.HBM))


def stage_kernel(ints_hbm, after, ints_ref, staged_ref, sem):
    del after
    staged_ref[...] = jnp.zeros_like(staged_ref)
    rows = ints_hbm.shape[0] // STAGE_COPIES
    copies = [
        pltpu.make_async_copy(
            ints_hbm.at[pl.ds(part * rows, rows), :], ints_ref.at[pl.ds(part * rows, rows), :], sem.at[part]
        )
        for part in range(STAGE_COPIES)
    ]
    for copy in copies:
        copy.start()
    for copy in copies:
        copy.wait()


def stage(integrals, after):
    return pl.pallas_call(
        stage_kernel,
        out_shape=[pltpu.VMEM(integrals.shape, integrals.dtype), jax.ShapeDtypeStruct((8, 128), jnp.float32)],
        in_specs=[pl.BlockSpec(memory_space=pltpu.HBM), pl.BlockSpec(memory_space=pl.ANY)],
        out_specs=[WHOLE] * 2,
        scratch_shapes=[pltpu.SemaphoreType.DMA((STAGE_COPIES,))],
        compiler_params=pltpu.CompilerParams(vmem_limit_bytes=SMALL_VMEM),
        cost_estimate=LIGHT,
        name="stage_integrals",
    )(pltpu.with_memory_space_constraint(integrals, pltpu.HBM), after)


def lay_out(near, other_ref, panel):
    depth = other_ref.shape[2]
    own = lax.rem(lax.axis_index("pan"), 2 * other_ref.shape[0])
    for step in range(2 * other_ref.shape[0]):
        held = other_ref[step // 2] if step % 2 else near[step // 2][...]
        panel[:, pl.ds(pl.multiple_of((own ^ step) * depth, depth), depth)] = held


def int_keep(screen_ref, ints_shape, pair_size):
    in_pair = lax.axis_index("grp") * ints_shape[0] // pair_size
    out_pair = lax.axis_index("pan") * ints_shape[1] // pair_size
    return screen_ref[in_pair, out_pair].astype(jnp.float32)


def product_blocks(panel, ints_ref):
    row_step = min(ROW_TILE, panel.shape[0])
    return [
        (row, column)
        for column in range(0, ints_ref.shape[1], COLUMN_TILE)
        for row in range(0, panel.shape[0], row_step)
    ]


def block_sums(panel, ints_ref, row, column):
    rows = slice(row, row + min(ROW_TILE, panel.shape[0]))
    ints = ints_ref[:, column : column + COLUMN_TILE]
    return jnp.dot(panel[rows, :], ints, preferred_element_type=jnp.float32)


def own_kernel(pair_size, int_screen_ref, near_ref, other_ref, ints_ref, *refs):
    sum_ref, panel = refs[-2:]
    keep = int_keep(int_screen_ref, ints_ref.shape, pair_size)
    lay_out([near_ref.at[place] for place in range(near_ref.shape[0])], other_ref, panel)
    for row, column in product_blocks(panel, ints_ref):
        sums = block_sums(panel, ints_ref, row, column) * keep
        sum_ref[row : row + sums.shape[0], column : column + COLUMN_TILE] = sums


def away_kernel(pair_size, near_count, int_screen_ref, *refs):
    near, (other_ref, ints_ref, before_ref) = refs[:near_count], refs[near_count : near_count + 3]
    code_ref, scale_ref, panel = refs[-3:]
    keep = int_keep(int_screen_ref, ints_ref.shape, pair_size)
    lay_out(near, other_ref, panel)
    first = scale_ref.shape[0] - code_ref.shape[0] // TS
    if first:
        scale_ref[:first, :] = before_ref[...]
    for row, column in product_blocks(panel, ints_ref):
        sums = block_sums(panel, ints_ref, row, column) * keep
        columns = slice(column, column + COLUMN_TILE)
        for at in range(0, sums.shape[0], TS):
            slot, rows = first + (row + at) // TS, slice(row + at, row + at + TS)
            part = sums[at : at + TS]
            top = jnp.maximum(jnp.max(jnp.abs(part), axis=0, keepdims=True), LEAST_SCALE)
            code = jnp.round(part * (CODE_MAX / top))
            code_ref[rows, columns] = code.astype(jnp.int32).astype(jnp.int16)
            scale_ref[slot : slot + 1, columns] = top * (1.0 / CODE_MAX)


def product(kernel, int_screen, arrays, gates, row_count, ints, out_rows_types, name):
    int_count, ab_count = ints.shape
    return pl.pallas_call(
        kernel,
        out_shape=[jax.ShapeDtypeStruct((rows, ab_count), dtype) for rows, dtype in out_rows_types],
        in_specs=[pl.BlockSpec(memory_space=pltpu.SMEM)]
        + [WHOLE] * len(arrays)
        + [pl.BlockSpec(memory_space=pl.ANY)] * len(gates),
        out_specs=[WHOLE] * len(out_rows_types),
        scratch_shapes=[pltpu.VMEM((row_count, int_count), ints.dtype)],
        compiler_params=pltpu.CompilerParams(vmem_limit_bytes=PRODUCT_VMEM),
        cost_estimate=LIGHT,
        name=name,
    )(int_screen, *arrays, *gates)


def join_kernel(screen_ref, own_ref, scale_ref, *refs):
    code_refs, (out_ref, total) = refs[:-2], refs[-2:]
    grp_index = lax.axis_index("grp")
    first_tile = grp_index * BLOCK_TILES
    own_slots, own_count = live_slots(screen_ref, first_tile, grp_index)
    slots, count = live_slots(screen_ref, first_tile, 1 - grp_index)
    total[...] = jnp.zeros_like(total)
    for slot in range(LIVE_MAX):

        @pl.when(slot < own_count)
        def _():
            rows = pl.ds(pl.multiple_of(own_slots[slot] * TS, TS), TS)
            total[rows, :] = own_ref[slot * TS : (slot + 1) * TS, :]

    for (first, last), code_ref in zip(SLOT_CHUNKS, code_refs):
        for slot in range(first, last):

            @pl.when(slot < count)
            def _():
                rows = pl.ds(pl.multiple_of(slots[slot] * TS, TS), TS)
                code = code_ref[(slot - first) * TS : (slot - first + 1) * TS, :].astype(jnp.float32)
                total[rows, :] += code * scale_ref[slot : slot + 1, :]

    out_ref[...] = total[...].astype(out_ref.dtype)


def join(amp_screen, own_sum, scales, codes, row_count):
    ab_count = own_sum.shape[1]
    arrays = [own_sum, scales, *codes]

    def tall(rows):
        return pl.BlockSpec((rows, JOIN_TILE), lambda j: (0, j))

    return pl.pallas_call(
        join_kernel,
        grid=(ab_count // JOIN_TILE,),
        out_shape=jax.ShapeDtypeStruct((row_count, ab_count), jnp.bfloat16),
        in_specs=[pl.BlockSpec(memory_space=pltpu.SMEM)] + [tall(array.shape[0]) for array in arrays],
        out_specs=tall(row_count),
        scratch_shapes=[pltpu.VMEM((row_count, JOIN_TILE), jnp.float32)],
        compiler_params=pltpu.CompilerParams(vmem_limit_bytes=SMALL_VMEM),
        name="join",
    )(amp_screen, *arrays)


def routes(pan_count):
    half = pan_count // 2
    places = [(pan, grp) for pan in range(pan_count) for grp in range(2)]

    def at(pan, grp):
        return pan * 2 + grp

    def away(pan, grp):
        return pan // half != grp

    def flip(bits):
        return [(at(pan, grp), at(pan ^ bits, grp)) for pan, grp in places]

    first = [
        (at(pan, grp), at(pan, 1 - grp) if away(pan, grp) else at((pan + half) % pan_count, grp))
        for pan, grp in places
    ]
    across = [
        (at(pan, grp), at((pan + half) % pan_count, 1 - grp) if away(pan, grp) else at(pan ^ 1, grp))
        for pan, grp in places
    ]
    swap = [(at(pan, grp), at(pan, 1 - grp)) for pan, grp in places]
    return first, across, swap, flip


def near_blocks(block, flip, block_count):
    return [block] + [lax.ppermute(block, AXES, flip(bits)) for bits in range(2, block_count, 2)]


def two_group_shards(pan_count, amplitudes, integrals, amp_screen, int_screen):
    pair_size = TS * TS
    row_count, col_count = amplitudes.shape
    block_count = integrals.shape[0] // col_count
    if (
        row_count != BLOCK_TILES * TS
        or amp_screen.shape[1] != 2
        or integrals.shape[0] != pair_size
        or block_count * 2 != pan_count
    ):
        return shards(amplitudes, integrals, amp_screen, int_screen)
    first, across, swap, flip = routes(pan_count)
    is_own = lax.axis_index("pan") // (pan_count // 2) == lax.axis_index("grp")

    amp_screen = amp_screen.T
    picked = pick_live(amplitudes, amp_screen, pair_size)

    def away_product(near, before, gates):
        other = lax.ppermute(jnp.stack(near), AXES, flip(1))
        rows = near[0].shape[0]
        scale_rows = rows // TS + (0 if before is None else before.shape[0])
        before = gates[0] if before is None else before
        return product(
            functools.partial(away_kernel, pair_size, len(near)), int_screen, [*near, other, ints, before], gates,
            rows, ints, ((rows, jnp.int16), (scale_rows, jnp.float32)), "away_product",
        )

    arrived = [(lax.ppermute(part, AXES, first), lax.ppermute(part, AXES, across)) for part in picked]
    own_block = jnp.concatenate([jnp.where(is_own, part, pair[0]) for part, pair in zip(picked, arrived)], axis=0)
    away_a, away_b = [jnp.where(is_own, *pair) for pair in arrived]
    ints, staged = stage(integrals, away_a)

    near_a = near_blocks(away_a, flip, block_count)
    near_a, staged = lax.optimization_barrier((near_a, staged))
    away_b, near_a = lax.optimization_barrier((away_b, near_a))
    near_b = near_blocks(away_b, flip, block_count)
    code_a, scale_a = away_product(near_a, None, [staged])
    came_a = lax.ppermute(code_a, AXES, swap)
    near_b, scale_a = lax.optimization_barrier((near_b, scale_a))
    own_block, near_b = lax.optimization_barrier((own_block, near_b))
    own_near = near_blocks(own_block, flip, block_count)
    code_b, scales = away_product(near_b, scale_a, [])
    came_b, came_scales = lax.ppermute(code_b, AXES, swap), lax.ppermute(scales, AXES, swap)
    own_other = jnp.stack([lax.ppermute(block, AXES, flip(1)) for block in own_near])
    (own_sum,) = product(
        functools.partial(own_kernel, pair_size), int_screen, [jnp.stack(own_near), own_other, ints], [],
        own_block.shape[0], ints, ((own_block.shape[0], jnp.float32),), "own_product",
    )
    return join(amp_screen, own_sum, came_scales, (came_a, came_b), row_count)


def column_pairs(piece_width, pair_size, pair_count):
    col_pair = jnp.arange(piece_width) // pair_size
    return (col_pair[None, :] == jnp.arange(pair_count)[:, None]).astype(jnp.bfloat16)


def shards(amplitudes, integrals, amp_screen, int_screen):
    pair_size = TS * TS
    row_count, col_count = amplitudes.shape
    int_count, ab_count = integrals.shape
    tile_count = row_count // TS
    pair_count = amp_screen.shape[1]
    grp_index = lax.axis_index("grp")
    pan_index = lax.axis_index("pan")
    screen_rows = lax.dynamic_slice_in_dim(amp_screen, grp_index * tile_count, tile_count, 0)
    in_pair = grp_index * int_count // pair_size
    out_pair = pan_index * ab_count // pair_size
    int_keep = int_screen[in_pair, out_pair].astype(jnp.bfloat16)
    int_panel = lax.all_gather(integrals * int_keep, "grp", axis=0, tiled=True)
    panel = lax.all_gather(amplitudes, "pan", axis=1, tiled=True)
    piece_width = panel.shape[1]
    onehot = column_pairs(piece_width, pair_size, pair_count)
    keep_mask = jnp.dot(
        screen_rows.astype(jnp.bfloat16), onehot, preferred_element_type=jnp.float32
    ).astype(jnp.bfloat16)
    masked = (panel.reshape(tile_count, TS, piece_width) * keep_mask[:, None, :]).reshape(
        row_count, piece_width
    )
    summed = jnp.dot(masked, int_panel, preferred_element_type=jnp.float32)
    return summed.astype(jnp.bfloat16)


def solution(mesh):
    in_specs = (P("grp", "pan"), P("grp", "pan"), P(), P())
    out_specs = P("grp", "pan")
    pan_count, grp_count = mesh.shape["pan"], mesh.shape["grp"]
    body = shards
    if grp_count == 2 and pan_count >= 4 and pan_count & (pan_count - 1) == 0:
        body = functools.partial(two_group_shards, pan_count)
    return jax.shard_map(body, mesh=mesh, in_specs=in_specs, out_specs=out_specs, check_vma=False)
```

```python
import functools

import jax
import jax.numpy as jnp
from jax import lax
from jax.experimental import pallas as pl
from jax.experimental.pallas import tpu as pltpu
from jax.sharding import PartitionSpec as P

TS = 64
LIVE_MAX = 4
BLOCK_TILES = 8
AXES = ("pan", "grp")
SLOT_CHUNKS = ((0, 2), (2, 4))
CODE_MAX = 32767.0
STAGE_COPIES = 8
LEAST_SCALE = 1e-33
ROW_TILE = 128
COLUMN_TILE = 256
JOIN_TILE = 512
SMALL_VMEM = 8 * 1024 * 1024
PRODUCT_VMEM = 16 * 1024 * 1024
LIGHT = pl.CostEstimate(flops=1, bytes_accessed=1, transcendentals=0)
WHOLE = pl.BlockSpec(memory_space=pltpu.VMEM)


def live_slots(screen_ref, first_tile, column):
    count = jnp.int32(0)
    slots = [jnp.int32(0)] * LIVE_MAX
    for tile in range(BLOCK_TILES):
        live = screen_ref[column, first_tile + tile] != 0
        for slot in range(LIVE_MAX):
            slots[slot] = jnp.where(live & (count == slot), tile, slots[slot])
        count = count + live.astype(jnp.int32)
    return slots, count


def pick_kernel(pair_size, screen_hbm, amps_hbm, *rest):
    picked_refs, (screen_ref, amps_ref, sem) = rest[:-3], rest[-3:]
    screen_copy = pltpu.make_async_copy(screen_hbm, screen_ref, sem.at[0])
    amps_copy = pltpu.make_async_copy(amps_hbm, amps_ref, sem.at[1])
    screen_copy.start()
    amps_copy.start()
    screen_copy.wait()
    column = lax.axis_index("pan") * amps_ref.shape[1] // pair_size
    slots, _ = live_slots(screen_ref, lax.axis_index("grp") * BLOCK_TILES, column)
    amps_copy.wait()
    for (first, last), picked_ref in zip(SLOT_CHUNKS, picked_refs):
        for slot in range(first, last):
            rows = pl.ds(pl.multiple_of(slots[slot] * TS, TS), TS)
            picked_ref[(slot - first) * TS : (slot - first + 1) * TS, :] = amps_ref[rows, :]


def pick_live(amplitudes, amp_screen, pair_size):
    return pl.pallas_call(
        functools.partial(pick_kernel, pair_size),
        out_shape=[
            jax.ShapeDtypeStruct(((last - first) * TS, amplitudes.shape[1]), amplitudes.dtype)
            for first, last in SLOT_CHUNKS
        ],
        in_specs=[pl.BlockSpec(memory_space=pltpu.HBM)] * 2,
        out_specs=[WHOLE] * len(SLOT_CHUNKS),
        scratch_shapes=[
            pltpu.SMEM(amp_screen.shape, amp_screen.dtype),
            pltpu.VMEM(amplitudes.shape, amplitudes.dtype),
            pltpu.SemaphoreType.DMA((2,)),
        ],
        compiler_params=pltpu.CompilerParams(vmem_limit_bytes=SMALL_VMEM),
        name="pick_live",
    )(in_hbm(amp_screen), in_hbm(amplitudes))


def in_hbm(array):
    return pltpu.with_memory_space_constraint(array, pltpu.HBM)


def stage_kernel(ints_hbm, after, ints_ref, staged_ref, sem):
    del after
    staged_ref[...] = jnp.zeros_like(staged_ref)
    rows = ints_hbm.shape[0] // STAGE_COPIES
    copies = [
        pltpu.make_async_copy(
            ints_hbm.at[pl.ds(part * rows, rows), :], ints_ref.at[pl.ds(part * rows, rows), :], sem.at[part]
        )
        for part in range(STAGE_COPIES)
    ]
    for copy in copies:
        copy.start()
    for copy in copies:
        copy.wait()


def stage(integrals, after):
    return pl.pallas_call(
        stage_kernel,
        out_shape=[pltpu.VMEM(integrals.shape, integrals.dtype), jax.ShapeDtypeStruct((8, 128), jnp.float32)],
        in_specs=[pl.BlockSpec(memory_space=pltpu.HBM), pl.BlockSpec(memory_space=pl.ANY)],
        out_specs=[WHOLE] * 2,
        scratch_shapes=[pltpu.SemaphoreType.DMA((STAGE_COPIES,))],
        compiler_params=pltpu.CompilerParams(vmem_limit_bytes=SMALL_VMEM),
        cost_estimate=LIGHT,
        name="stage_integrals",
    )(in_hbm(integrals), after)


def lay_out(near, other_ref, panel):
    depth = other_ref.shape[2]
    own = lax.rem(lax.axis_index("pan"), 2 * other_ref.shape[0])
    for step in range(2 * other_ref.shape[0]):
        held = other_ref[step // 2] if step % 2 else near[step // 2][...]
        panel[:, pl.ds(pl.multiple_of((own ^ step) * depth, depth), depth)] = held


def int_keep(screen_ref, ints_shape, pair_size):
    in_pair = lax.axis_index("grp") * ints_shape[0] // pair_size
    out_pair = lax.axis_index("pan") * ints_shape[1] // pair_size
    return screen_ref[in_pair, out_pair].astype(jnp.float32)


def product_blocks(panel, ints_ref):
    row_step = min(ROW_TILE, panel.shape[0])
    return [
        (row, column)
        for column in range(0, ints_ref.shape[1], COLUMN_TILE)
        for row in range(0, panel.shape[0], row_step)
    ]


def block_sums(panel, ints_ref, row, column):
    rows = slice(row, row + min(ROW_TILE, panel.shape[0]))
    ints = ints_ref[:, column : column + COLUMN_TILE]
    return jnp.dot(panel[rows, :], ints, preferred_element_type=jnp.float32)


def own_kernel(pair_size, int_screen_ref, near_ref, other_ref, ints_ref, *refs):
    sum_ref, panel = refs[-2:]
    keep = int_keep(int_screen_ref, ints_ref.shape, pair_size)
    lay_out([near_ref.at[place] for place in range(near_ref.shape[0])], other_ref, panel)
    for row, column in product_blocks(panel, ints_ref):
        sums = block_sums(panel, ints_ref, row, column) * keep
        sum_ref[row : row + sums.shape[0], column : column + COLUMN_TILE] = sums


def away_kernel(pair_size, near_count, int_screen_ref, *refs):
    near, (other_ref, ints_ref, before_ref) = refs[:near_count], refs[near_count : near_count + 3]
    code_ref, scale_ref, panel = refs[-3:]
    keep = int_keep(int_screen_ref, ints_ref.shape, pair_size)
    lay_out(near, other_ref, panel)
    first = scale_ref.shape[0] - code_ref.shape[0] // TS
    if first:
        scale_ref[:first, :] = before_ref[...]
    for row, column in product_blocks(panel, ints_ref):
        sums = block_sums(panel, ints_ref, row, column) * keep
        columns = slice(column, column + COLUMN_TILE)
        for at in range(0, sums.shape[0], TS):
            slot, rows = first + (row + at) // TS, slice(row + at, row + at + TS)
            part = sums[at : at + TS]
            top = jnp.maximum(jnp.max(jnp.abs(part), axis=0, keepdims=True), LEAST_SCALE)
            code = jnp.round(part * (CODE_MAX / top))
            code_ref[rows, columns] = code.astype(jnp.int32).astype(jnp.int16)
            scale_ref[slot : slot + 1, columns] = top * (1.0 / CODE_MAX)


def product(kernel, int_screen, arrays, gates, row_count, ints, out_rows_types, name):
    int_count, ab_count = ints.shape
    return pl.pallas_call(
        kernel,
        out_shape=[jax.ShapeDtypeStruct((rows, ab_count), dtype) for rows, dtype in out_rows_types],
        in_specs=[pl.BlockSpec(memory_space=pltpu.SMEM)]
        + [WHOLE] * len(arrays)
        + [pl.BlockSpec(memory_space=pl.ANY)] * len(gates),
        out_specs=[WHOLE] * len(out_rows_types),
        scratch_shapes=[pltpu.VMEM((row_count, int_count), ints.dtype)],
        compiler_params=pltpu.CompilerParams(vmem_limit_bytes=PRODUCT_VMEM),
        cost_estimate=LIGHT,
        name=name,
    )(int_screen, *arrays, *gates)


def join_kernel(screen_ref, own_ref, scale_ref, *refs):
    code_refs, (out_hbm, held, sem) = refs[: len(SLOT_CHUNKS)], refs[len(SLOT_CHUNKS) :]
    grp_index = lax.axis_index("grp")
    first_tile = grp_index * BLOCK_TILES
    own_slots, own_count = live_slots(screen_ref, first_tile, grp_index)
    slots, count = live_slots(screen_ref, first_tile, 1 - grp_index)

    def tile_rows(slot):
        return pl.ds(pl.multiple_of(slot * TS, TS), TS)

    copies = []
    for part in range(own_ref.shape[1] // JOIN_TILE):
        columns = slice(part * JOIN_TILE, (part + 1) * JOIN_TILE)
        held_part = held.at[part]
        held_part[...] = jnp.zeros_like(held_part)
        for slot in range(LIVE_MAX):

            @pl.when(slot < own_count)
            def _():
                held_part[tile_rows(own_slots[slot]), :] = own_ref[slot * TS : (slot + 1) * TS, columns].astype(held.dtype)

        for (first, last), code_ref in zip(SLOT_CHUNKS, code_refs):
            for slot in range(first, last):

                @pl.when(slot < count)
                def _():
                    code = code_ref[(slot - first) * TS : (slot - first + 1) * TS, columns].astype(jnp.float32)
                    away = code * scale_ref[slot : slot + 1, columns]
                    at = jnp.int32(-1)
                    for own_slot in range(LIVE_MAX):
                        at = jnp.where((own_slot < own_count) & (own_slots[own_slot] == slots[slot]), own_slot, at)
                    own = own_ref[tile_rows(jnp.maximum(at, 0)), columns]
                    total = away + jnp.where(at >= 0, own, 0.0)
                    held_part[tile_rows(slots[slot]), :] = total.astype(held.dtype)

        copies.append(pltpu.make_async_copy(held_part, out_hbm.at[:, columns], sem.at[part]))
        copies[-1].start()
    for copy in copies:
        copy.wait()


def join(amp_screen, own_sum, scales, codes, row_count):
    ab_count = own_sum.shape[1]
    arrays = [own_sum, scales, *codes]
    return pl.pallas_call(
        join_kernel,
        out_shape=jax.ShapeDtypeStruct((row_count, ab_count), jnp.bfloat16),
        in_specs=[pl.BlockSpec(memory_space=pltpu.SMEM)] + [WHOLE] * len(arrays),
        out_specs=pl.BlockSpec(memory_space=pltpu.HBM),
        scratch_shapes=[
            pltpu.VMEM((ab_count // JOIN_TILE, row_count, JOIN_TILE), jnp.bfloat16),
            pltpu.SemaphoreType.DMA((ab_count // JOIN_TILE,)),
        ],
        compiler_params=pltpu.CompilerParams(vmem_limit_bytes=PRODUCT_VMEM),
        name="join",
    )(amp_screen, *arrays)


def routes(pan_count):
    half = pan_count // 2
    places = [(pan, grp) for pan in range(pan_count) for grp in range(2)]

    def at(pan, grp):
        return pan * 2 + grp

    def away(pan, grp):
        return pan // half != grp

    def flip(bits):
        return [(at(pan, grp), at(pan ^ bits, grp)) for pan, grp in places]

    first = [
        (at(pan, grp), at(pan, 1 - grp) if away(pan, grp) else at((pan + half) % pan_count, grp))
        for pan, grp in places
    ]
    across = [
        (at(pan, grp), at((pan + half) % pan_count, 1 - grp) if away(pan, grp) else at(pan ^ 1, grp))
        for pan, grp in places
    ]
    swap = [(at(pan, grp), at(pan, 1 - grp)) for pan, grp in places]
    return first, across, swap, flip


def near_blocks(block, flip, block_count):
    return [block] + [lax.ppermute(block, AXES, flip(bits)) for bits in range(2, block_count, 2)]


def two_group_shards(pan_count, amplitudes, integrals, amp_screen, int_screen):
    pair_size = TS * TS
    row_count, col_count = amplitudes.shape
    block_count = integrals.shape[0] // col_count
    if (
        row_count != BLOCK_TILES * TS
        or amp_screen.shape[1] != 2
        or integrals.shape[0] != pair_size
        or block_count * 2 != pan_count
    ):
        return shards(amplitudes, integrals, amp_screen, int_screen)
    first, across, swap, flip = routes(pan_count)
    is_own = lax.axis_index("pan") // (pan_count // 2) == lax.axis_index("grp")

    amp_screen = amp_screen.T
    picked = pick_live(amplitudes, amp_screen, pair_size)

    def away_product(near, before, gates):
        other = lax.ppermute(jnp.stack(near), AXES, flip(1))
        rows = near[0].shape[0]
        scale_rows = rows // TS + (0 if before is None else before.shape[0])
        before = gates[0] if before is None else before
        return product(
            functools.partial(away_kernel, pair_size, len(near)), int_screen, [*near, other, ints, before], gates,
            rows, ints, ((rows, jnp.int16), (scale_rows, jnp.float32)), "away_product",
        )

    arrived = [(lax.ppermute(part, AXES, first), lax.ppermute(part, AXES, across)) for part in picked]
    own_block = jnp.concatenate([jnp.where(is_own, part, pair[0]) for part, pair in zip(picked, arrived)], axis=0)
    away_a, away_b = [jnp.where(is_own, *pair) for pair in arrived]
    ints, staged = stage(integrals, away_a)

    near_a = near_blocks(away_a, flip, block_count)
    near_a, staged = lax.optimization_barrier((near_a, staged))
    away_b, near_a = lax.optimization_barrier((away_b, near_a))
    near_b = near_blocks(away_b, flip, block_count)
    code_a, scale_a = away_product(near_a, None, [staged])
    came_a = lax.ppermute(code_a, AXES, swap)
    near_b, scale_a = lax.optimization_barrier((near_b, scale_a))
    own_block, near_b = lax.optimization_barrier((own_block, near_b))
    own_near = near_blocks(own_block, flip, block_count)
    code_b, scales = away_product(near_b, scale_a, [])
    came_b, came_scales = lax.ppermute(code_b, AXES, swap), lax.ppermute(scales, AXES, swap)
    own_near, came_a = lax.optimization_barrier((own_near, came_a))
    own_other = jnp.stack([lax.ppermute(block, AXES, flip(1)) for block in own_near])
    (own_sum,) = product(
        functools.partial(own_kernel, pair_size), int_screen, [jnp.stack(own_near), own_other, ints], [],
        own_block.shape[0], ints, ((own_block.shape[0], jnp.float32),), "own_product",
    )
    return join(amp_screen, own_sum, came_scales, (came_a, came_b), row_count)


def column_pairs(piece_width, pair_size, pair_count):
    col_pair = jnp.arange(piece_width) // pair_size
    return (col_pair[None, :] == jnp.arange(pair_count)[:, None]).astype(jnp.bfloat16)


def shards(amplitudes, integrals, amp_screen, int_screen):
    pair_size = TS * TS
    row_count, col_count = amplitudes.shape
    int_count, ab_count = integrals.shape
    tile_count = row_count // TS
    pair_count = amp_screen.shape[1]
    grp_index = lax.axis_index("grp")
    pan_index = lax.axis_index("pan")
    screen_rows = lax.dynamic_slice_in_dim(amp_screen, grp_index * tile_count, tile_count, 0)
    in_pair = grp_index * int_count // pair_size
    out_pair = pan_index * ab_count // pair_size
    int_keep = int_screen[in_pair, out_pair].astype(jnp.bfloat16)
    int_panel = lax.all_gather(integrals * int_keep, "grp", axis=0, tiled=True)
    panel = lax.all_gather(amplitudes, "pan", axis=1, tiled=True)
    piece_width = panel.shape[1]
    onehot = column_pairs(piece_width, pair_size, pair_count)
    keep_mask = jnp.dot(
        screen_rows.astype(jnp.bfloat16), onehot, preferred_element_type=jnp.float32
    ).astype(jnp.bfloat16)
    masked = (panel.reshape(tile_count, TS, piece_width) * keep_mask[:, None, :]).reshape(
        row_count, piece_width
    )
    summed = jnp.dot(masked, int_panel, preferred_element_type=jnp.float32)
    return summed.astype(jnp.bfloat16)


def solution(mesh):
    in_specs = (P("grp", "pan"), P("grp", "pan"), P(), P())
    out_specs = P("grp", "pan")
    pan_count, grp_count = mesh.shape["pan"], mesh.shape["grp"]
    body = shards
    if grp_count == 2 and pan_count >= 4 and pan_count & (pan_count - 1) == 0:
        body = functools.partial(two_group_shards, pan_count)
    return jax.shard_map(body, mesh=mesh, in_specs=in_specs, out_specs=out_specs, check_vma=False)
```

```python
import functools

import jax
import jax.numpy as jnp
from jax import lax
from jax.experimental import pallas as pl
from jax.experimental.pallas import tpu as pltpu
from jax.sharding import PartitionSpec as P

TS = 64
LIVE_MAX = 4
BLOCK_TILES = 8
AXES = ("pan", "grp")
SLOT_CHUNKS = ((0, 2), (2, 4))
CODE_MAX = 32767.0
STAGE_COPIES = 8
LEAST_SCALE = 1e-33
ROW_TILE = 128
COLUMN_TILE = 256
JOIN_TILE = 512
SMALL_VMEM = 8 * 1024 * 1024
PRODUCT_VMEM = 16 * 1024 * 1024
LIGHT = pl.CostEstimate(flops=1, bytes_accessed=1, transcendentals=0)
WHOLE = pl.BlockSpec(memory_space=pltpu.VMEM)


def live_slots(screen_ref, first_tile, column):
    count = jnp.int32(0)
    slots = [jnp.int32(0)] * LIVE_MAX
    for tile in range(BLOCK_TILES):
        live = screen_ref[column, first_tile + tile] != 0
        for slot in range(LIVE_MAX):
            slots[slot] = jnp.where(live & (count == slot), tile, slots[slot])
        count = count + live.astype(jnp.int32)
    return slots, count


def pick_kernel(pair_size, screen_hbm, amps_hbm, *rest):
    picked_refs, (screen_ref, amps_ref, sem) = rest[:-3], rest[-3:]
    screen_copy = pltpu.make_async_copy(screen_hbm, screen_ref, sem.at[0])
    amps_copy = pltpu.make_async_copy(amps_hbm, amps_ref, sem.at[1])
    screen_copy.start()
    amps_copy.start()
    screen_copy.wait()
    column = lax.axis_index("pan") * amps_ref.shape[1] // pair_size
    slots, _ = live_slots(screen_ref, lax.axis_index("grp") * BLOCK_TILES, column)
    amps_copy.wait()
    for (first, last), picked_ref in zip(SLOT_CHUNKS, picked_refs):
        for slot in range(first, last):
            rows = pl.ds(pl.multiple_of(slots[slot] * TS, TS), TS)
            picked_ref[(slot - first) * TS : (slot - first + 1) * TS, :] = amps_ref[rows, :]


def pick_live(amplitudes, amp_screen, pair_size):
    return pl.pallas_call(
        functools.partial(pick_kernel, pair_size),
        out_shape=[
            jax.ShapeDtypeStruct(((last - first) * TS, amplitudes.shape[1]), amplitudes.dtype)
            for first, last in SLOT_CHUNKS
        ],
        in_specs=[pl.BlockSpec(memory_space=pltpu.HBM)] * 2,
        out_specs=[WHOLE] * len(SLOT_CHUNKS),
        scratch_shapes=[
            pltpu.SMEM(amp_screen.shape, amp_screen.dtype),
            pltpu.VMEM(amplitudes.shape, amplitudes.dtype),
            pltpu.SemaphoreType.DMA((2,)),
        ],
        compiler_params=pltpu.CompilerParams(vmem_limit_bytes=SMALL_VMEM),
        name="pick_live",
    )(in_hbm(amp_screen), in_hbm(amplitudes))


def in_hbm(array):
    return pltpu.with_memory_space_constraint(array, pltpu.HBM)


def stage_kernel(ints_hbm, after, ints_ref, staged_ref, sem):
    del after
    staged_ref[...] = jnp.zeros_like(staged_ref)
    rows = ints_hbm.shape[0] // STAGE_COPIES
    copies = [
        pltpu.make_async_copy(
            ints_hbm.at[pl.ds(part * rows, rows), :], ints_ref.at[pl.ds(part * rows, rows), :], sem.at[part]
        )
        for part in range(STAGE_COPIES)
    ]
    for copy in copies:
        copy.start()
    for copy in copies:
        copy.wait()


def stage(integrals, after):
    return pl.pallas_call(
        stage_kernel,
        out_shape=[pltpu.VMEM(integrals.shape, integrals.dtype), jax.ShapeDtypeStruct((8, 128), jnp.float32)],
        in_specs=[pl.BlockSpec(memory_space=pltpu.HBM), pl.BlockSpec(memory_space=pl.ANY)],
        out_specs=[WHOLE] * 2,
        scratch_shapes=[pltpu.SemaphoreType.DMA((STAGE_COPIES,))],
        compiler_params=pltpu.CompilerParams(vmem_limit_bytes=SMALL_VMEM),
        cost_estimate=LIGHT,
        name="stage_integrals",
    )(in_hbm(integrals), after)


def lay_out(near, other, panel):
    depth = near[0].shape[1]
    own = lax.rem(lax.axis_index("pan"), 2 * len(near))
    for step in range(2 * len(near)):
        held = (other if step % 2 else near)[step // 2][...]
        panel[:, pl.ds(pl.multiple_of((own ^ step) * depth, depth), depth)] = held


def int_keep(screen_ref, ints_shape, pair_size):
    in_pair = lax.axis_index("grp") * ints_shape[0] // pair_size
    out_pair = lax.axis_index("pan") * ints_shape[1] // pair_size
    return screen_ref[in_pair, out_pair].astype(jnp.float32)


def product_blocks(panel, ints_ref):
    row_step = min(ROW_TILE, panel.shape[0])
    return [
        (row, column)
        for column in range(0, ints_ref.shape[1], COLUMN_TILE)
        for row in range(0, panel.shape[0], row_step)
    ]


def block_sums(panel, ints_ref, row, column):
    rows = slice(row, row + min(ROW_TILE, panel.shape[0]))
    ints = ints_ref[:, column : column + COLUMN_TILE]
    return jnp.dot(panel[rows, :], ints, preferred_element_type=jnp.float32)


def own_kernel(pair_size, near_count, part, int_screen_ref, *refs):
    near, other, refs = refs[:near_count], refs[near_count : 2 * near_count], refs[2 * near_count :]
    ints_ref, (sum_ref, panel) = refs[0], refs[-2:]
    keep = int_keep(int_screen_ref, ints_ref.shape, pair_size)
    depth, width = near[0].shape[1], panel.shape[1]
    own = lax.rem(lax.axis_index("pan"), ints_ref.shape[0] // depth)
    half = (own // (2 * near_count)) ^ part
    for at in range(2 * near_count):
        held = (other if at % 2 else near)[at // 2][...]
        column = lax.rem(own ^ at, 2 * near_count) * depth
        panel[:, pl.ds(pl.multiple_of(column, depth), depth)] = held
    depth_rows = pl.ds(pl.multiple_of(half * width, width), width)
    for row, column in product_blocks(panel, ints_ref):
        rows, columns = slice(row, row + min(ROW_TILE, panel.shape[0])), slice(column, column + COLUMN_TILE)
        sums = jnp.dot(panel[rows, :], ints_ref[depth_rows, columns], preferred_element_type=jnp.float32)
        if part:
            sums = sums + refs[1][rows, columns]
        sum_ref[rows, columns] = sums * keep if part else sums


def away_kernel(pair_size, near_count, int_screen_ref, *refs):
    near, refs = refs[:near_count], refs[near_count:]
    other, refs = (refs[0], refs[1:]) if refs[0].ndim == 3 else (refs[:near_count], refs[near_count:])
    other = [other.at[place] for place in range(near_count)] if not isinstance(other, (tuple, list)) else other
    ints_ref, before_ref = refs[:2]
    code_ref, scale_ref, panel = refs[-3:]
    keep = int_keep(int_screen_ref, ints_ref.shape, pair_size)
    lay_out(near, other, panel)
    first = scale_ref.shape[0] - code_ref.shape[0] // TS
    if first:
        scale_ref[:first, :] = before_ref[...]
    for row, column in product_blocks(panel, ints_ref):
        sums = block_sums(panel, ints_ref, row, column) * keep
        columns = slice(column, column + COLUMN_TILE)
        for at in range(0, sums.shape[0], TS):
            slot, rows = first + (row + at) // TS, slice(row + at, row + at + TS)
            part = sums[at : at + TS]
            top = jnp.maximum(jnp.max(jnp.abs(part), axis=0, keepdims=True), LEAST_SCALE)
            code = jnp.round(part * (CODE_MAX / top))
            code_ref[rows, columns] = code.astype(jnp.int32).astype(jnp.int16)
            scale_ref[slot : slot + 1, columns] = top * (1.0 / CODE_MAX)


def product(kernel, int_screen, arrays, gates, row_count, ints, out_rows_types, name, parts=1):
    int_count, ab_count = ints.shape
    return pl.pallas_call(
        kernel,
        out_shape=[jax.ShapeDtypeStruct((rows, ab_count), dtype) for rows, dtype in out_rows_types],
        in_specs=[pl.BlockSpec(memory_space=pltpu.SMEM)]
        + [WHOLE] * len(arrays)
        + [pl.BlockSpec(memory_space=pl.ANY)] * len(gates),
        out_specs=[WHOLE] * len(out_rows_types),
        scratch_shapes=[pltpu.VMEM((row_count, int_count // parts), ints.dtype)],
        compiler_params=pltpu.CompilerParams(vmem_limit_bytes=PRODUCT_VMEM),
        cost_estimate=LIGHT,
        name=name,
    )(int_screen, *arrays, *gates)


def join_kernel(screen_ref, own_ref, scale_ref, *refs):
    code_refs, (out_hbm, held, sem) = refs[: len(SLOT_CHUNKS)], refs[len(SLOT_CHUNKS) :]
    grp_index = lax.axis_index("grp")
    first_tile = grp_index * BLOCK_TILES
    own_slots, own_count = live_slots(screen_ref, first_tile, grp_index)
    slots, count = live_slots(screen_ref, first_tile, 1 - grp_index)

    def tile_rows(slot):
        return pl.ds(pl.multiple_of(slot * TS, TS), TS)

    copies = []
    for part in range(own_ref.shape[1] // JOIN_TILE):
        columns = slice(part * JOIN_TILE, (part + 1) * JOIN_TILE)
        held_part = held.at[part]
        held_part[...] = jnp.zeros_like(held_part)
        for slot in range(LIVE_MAX):

            @pl.when(slot < own_count)
            def _():
                held_part[tile_rows(own_slots[slot]), :] = own_ref[slot * TS : (slot + 1) * TS, columns].astype(held.dtype)

        for (first, last), code_ref in zip(SLOT_CHUNKS, code_refs):
            for slot in range(first, last):

                @pl.when(slot < count)
                def _():
                    code = code_ref[(slot - first) * TS : (slot - first + 1) * TS, columns].astype(jnp.float32)
                    away = code * scale_ref[slot : slot + 1, columns]
                    at = jnp.int32(-1)
                    for own_slot in range(LIVE_MAX):
                        at = jnp.where((own_slot < own_count) & (own_slots[own_slot] == slots[slot]), own_slot, at)
                    own = own_ref[tile_rows(jnp.maximum(at, 0)), columns]
                    total = away + jnp.where(at >= 0, own, 0.0)
                    held_part[tile_rows(slots[slot]), :] = total.astype(held.dtype)

        copies.append(pltpu.make_async_copy(held_part, out_hbm.at[:, columns], sem.at[part]))
        copies[-1].start()
    for copy in copies:
        copy.wait()


def join(amp_screen, own_sum, scales, codes, row_count):
    ab_count = own_sum.shape[1]
    arrays = [own_sum, scales, *codes]
    return pl.pallas_call(
        join_kernel,
        out_shape=jax.ShapeDtypeStruct((row_count, ab_count), jnp.bfloat16),
        in_specs=[pl.BlockSpec(memory_space=pltpu.SMEM)] + [WHOLE] * len(arrays),
        out_specs=pl.BlockSpec(memory_space=pltpu.HBM),
        scratch_shapes=[
            pltpu.VMEM((ab_count // JOIN_TILE, row_count, JOIN_TILE), jnp.bfloat16),
            pltpu.SemaphoreType.DMA((ab_count // JOIN_TILE,)),
        ],
        compiler_params=pltpu.CompilerParams(vmem_limit_bytes=PRODUCT_VMEM),
        name="join",
    )(amp_screen, *arrays)


def routes(pan_count):
    half = pan_count // 2
    places = [(pan, grp) for pan in range(pan_count) for grp in range(2)]

    def at(pan, grp):
        return pan * 2 + grp

    def away(pan, grp):
        return pan // half != grp

    def flip(bits):
        return [(at(pan, grp), at(pan ^ bits, grp)) for pan, grp in places]

    first = [
        (at(pan, grp), at(pan, 1 - grp) if away(pan, grp) else at((pan + half) % pan_count, grp))
        for pan, grp in places
    ]
    across = [
        (at(pan, grp), at((pan + half) % pan_count, 1 - grp) if away(pan, grp) else at(pan ^ 1, grp))
        for pan, grp in places
    ]
    swap = [(at(pan, grp), at(pan, 1 - grp)) for pan, grp in places]
    return first, across, swap, flip


def near_blocks(block, flip, block_count):
    return [block] + [lax.ppermute(block, AXES, flip(bits)) for bits in range(2, block_count, 2)]


def two_group_shards(pan_count, amplitudes, integrals, amp_screen, int_screen):
    pair_size = TS * TS
    row_count, col_count = amplitudes.shape
    block_count = integrals.shape[0] // col_count
    if (
        row_count != BLOCK_TILES * TS
        or amp_screen.shape[1] != 2
        or integrals.shape[0] != pair_size
        or block_count * 2 != pan_count
    ):
        return shards(amplitudes, integrals, amp_screen, int_screen)
    first, across, swap, flip = routes(pan_count)
    is_own = lax.axis_index("pan") // (pan_count // 2) == lax.axis_index("grp")

    amp_screen = amp_screen.T
    picked = pick_live(amplitudes, amp_screen, pair_size)

    def crossed(near):
        return [lax.ppermute(block, AXES, flip(1)) for block in near]

    def away_product(near, other, before, gates):
        rows = near[0].shape[0]
        scale_rows = rows // TS + (0 if before is None else before.shape[0])
        before = gates[0] if before is None else before
        return product(
            functools.partial(away_kernel, pair_size, len(near)), int_screen, [*near, *other, ints, before], gates,
            rows, ints, ((rows, jnp.int16), (scale_rows, jnp.float32)), "away_product",
        )

    def own_half(near, before, part):
        rows = own_block.shape[0]
        return product(
            functools.partial(own_kernel, pair_size, len(near), part), int_screen,
            [*near, *crossed(near), ints, *before], [], rows, ints, ((rows, jnp.float32),), "own_product", 2,
        )[0]

    arrived = [(lax.ppermute(part, AXES, first), lax.ppermute(part, AXES, across)) for part in picked]
    own_block = jnp.concatenate([jnp.where(is_own, part, pair[0]) for part, pair in zip(picked, arrived)], axis=0)
    away_a, away_b = [jnp.where(is_own, *pair) for pair in arrived]
    ints, staged = stage(integrals, away_a)

    near_a = near_blocks(away_a, flip, block_count)
    near_a, staged = lax.optimization_barrier((near_a, staged))
    away_b, near_a = lax.optimization_barrier((away_b, near_a))
    other_a = [lax.ppermute(jnp.stack(near_a), AXES, flip(1))]
    code_a, scale_a = away_product(near_a, other_a, None, [staged])
    came_a = lax.ppermute(code_a, AXES, swap)
    near_b = near_blocks(away_b, flip, block_count)
    near_b, scale_a = lax.optimization_barrier((near_b, scale_a))
    own_block, near_b = lax.optimization_barrier((own_block, near_b))
    own_near = near_blocks(own_block, flip, block_count)
    code_b, scales = away_product(near_b, crossed(near_b), scale_a, [])
    came_b, came_scales = lax.ppermute(code_b, AXES, swap), lax.ppermute(scales, AXES, swap)
    half = len(own_near) // 2
    near_low, near_high = own_near[:half], own_near[half:]
    near_low, came_a = lax.optimization_barrier((near_low, came_a))
    own_sum = own_half(near_high, [own_half(near_low, [], 0)], 1)
    return join(amp_screen, own_sum, came_scales, (came_a, came_b), row_count)


def column_pairs(piece_width, pair_size, pair_count):
    col_pair = jnp.arange(piece_width) // pair_size
    return (col_pair[None, :] == jnp.arange(pair_count)[:, None]).astype(jnp.bfloat16)


def shards(amplitudes, integrals, amp_screen, int_screen):
    pair_size = TS * TS
    row_count, col_count = amplitudes.shape
    int_count, ab_count = integrals.shape
    tile_count = row_count // TS
    pair_count = amp_screen.shape[1]
    grp_index = lax.axis_index("grp")
    pan_index = lax.axis_index("pan")
    screen_rows = lax.dynamic_slice_in_dim(amp_screen, grp_index * tile_count, tile_count, 0)
    in_pair = grp_index * int_count // pair_size
    out_pair = pan_index * ab_count // pair_size
    int_keep = int_screen[in_pair, out_pair].astype(jnp.bfloat16)
    int_panel = lax.all_gather(integrals * int_keep, "grp", axis=0, tiled=True)
    panel = lax.all_gather(amplitudes, "pan", axis=1, tiled=True)
    piece_width = panel.shape[1]
    onehot = column_pairs(piece_width, pair_size, pair_count)
    keep_mask = jnp.dot(
        screen_rows.astype(jnp.bfloat16), onehot, preferred_element_type=jnp.float32
    ).astype(jnp.bfloat16)
    masked = (panel.reshape(tile_count, TS, piece_width) * keep_mask[:, None, :]).reshape(
        row_count, piece_width
    )
    summed = jnp.dot(masked, int_panel, preferred_element_type=jnp.float32)
    return summed.astype(jnp.bfloat16)


def solution(mesh):
    in_specs = (P("grp", "pan"), P("grp", "pan"), P(), P())
    out_specs = P("grp", "pan")
    pan_count, grp_count = mesh.shape["pan"], mesh.shape["grp"]
    body = shards
    if grp_count == 2 and pan_count >= 4 and pan_count & (pan_count - 1) == 0:
        body = functools.partial(two_group_shards, pan_count)
    return jax.shard_map(body, mesh=mesh, in_specs=in_specs, out_specs=out_specs, check_vma=False)
```

```python
import functools

import jax
import jax.numpy as jnp
from jax import lax
from jax.experimental import pallas as pl
from jax.experimental.pallas import tpu as pltpu
from jax.sharding import PartitionSpec as P

TS = 64
LIVE_MAX = 4
BLOCK_TILES = 8
AXES = ("pan", "grp")
SLOT_CHUNKS = ((0, 2), (2, 4))
CODE_MAX = 32767.0
DIGITS = 8192.0
SCALE_ROWS = 8
STAGE_COPIES = 8
LEAST_SCALE = 1e-33
ROW_TILE = 128
COLUMN_TILE = 256
JOIN_TILE = 512
SMALL_VMEM = 8 * 1024 * 1024
PRODUCT_VMEM = 16 * 1024 * 1024
LIGHT = pl.CostEstimate(flops=1, bytes_accessed=1, transcendentals=0)
MEDIUM = pl.CostEstimate(flops=1 << 30, bytes_accessed=1, transcendentals=0)
WHOLE = pl.BlockSpec(memory_space=pltpu.VMEM)


def live_slots(screen_ref, first_tile, column):
    count = jnp.int32(0)
    slots = [jnp.int32(0)] * LIVE_MAX
    for tile in range(BLOCK_TILES):
        live = screen_ref[column, first_tile + tile] != 0
        for slot in range(LIVE_MAX):
            slots[slot] = jnp.where(live & (count == slot), tile, slots[slot])
        count = count + live.astype(jnp.int32)
    return slots, count


def pick_kernel(pair_size, screen_hbm, amps_hbm, *rest):
    picked_refs, (screen_ref, amps_ref, sem) = rest[:-3], rest[-3:]
    screen_copy = pltpu.make_async_copy(screen_hbm, screen_ref, sem.at[0])
    amps_copy = pltpu.make_async_copy(amps_hbm, amps_ref, sem.at[1])
    screen_copy.start()
    amps_copy.start()
    screen_copy.wait()
    column = lax.axis_index("pan") * amps_ref.shape[1] // pair_size
    slots, _ = live_slots(screen_ref, lax.axis_index("grp") * BLOCK_TILES, column)
    amps_copy.wait()
    for (first, last), picked_ref in zip(SLOT_CHUNKS, picked_refs):
        for slot in range(first, last):
            rows = pl.ds(pl.multiple_of(slots[slot] * TS, TS), TS)
            picked_ref[(slot - first) * TS : (slot - first + 1) * TS, :] = amps_ref[rows, :]


def pick_live(amplitudes, amp_screen, pair_size):
    return pl.pallas_call(
        functools.partial(pick_kernel, pair_size),
        out_shape=[
            jax.ShapeDtypeStruct(((last - first) * TS, amplitudes.shape[1]), amplitudes.dtype)
            for first, last in SLOT_CHUNKS
        ],
        in_specs=[pl.BlockSpec(memory_space=pltpu.HBM)] * 2,
        out_specs=[WHOLE] * len(SLOT_CHUNKS),
        scratch_shapes=[
            pltpu.SMEM(amp_screen.shape, amp_screen.dtype),
            pltpu.VMEM(amplitudes.shape, amplitudes.dtype),
            pltpu.SemaphoreType.DMA((2,)),
        ],
        compiler_params=pltpu.CompilerParams(vmem_limit_bytes=SMALL_VMEM),
        name="pick_live",
    )(in_hbm(amp_screen), in_hbm(amplitudes))


def in_hbm(array):
    return pltpu.with_memory_space_constraint(array, pltpu.HBM)


def stage_kernel(ints_hbm, after, ints_ref, staged_ref, sem):
    del after
    staged_ref[...] = jnp.zeros_like(staged_ref)
    rows = ints_hbm.shape[0] // STAGE_COPIES
    copies = [
        pltpu.make_async_copy(
            ints_hbm.at[pl.ds(part * rows, rows), :], ints_ref.at[pl.ds(part * rows, rows), :], sem.at[part]
        )
        for part in range(STAGE_COPIES)
    ]
    for copy in copies:
        copy.start()
    for copy in copies:
        copy.wait()


def stage(integrals, after):
    return pl.pallas_call(
        stage_kernel,
        out_shape=[pltpu.VMEM(integrals.shape, integrals.dtype), jax.ShapeDtypeStruct((8, 128), jnp.float32)],
        in_specs=[pl.BlockSpec(memory_space=pltpu.HBM), pl.BlockSpec(memory_space=pl.ANY)],
        out_specs=[WHOLE] * 2,
        scratch_shapes=[pltpu.SemaphoreType.DMA((STAGE_COPIES,))],
        compiler_params=pltpu.CompilerParams(vmem_limit_bytes=SMALL_VMEM),
        cost_estimate=LIGHT,
        name="stage_integrals",
    )(in_hbm(integrals), after)


def lay_out(near, other, panel):
    depth = near[0].shape[1]
    own = lax.rem(lax.axis_index("pan"), 2 * len(near))
    for step in range(2 * len(near)):
        held = (other if step % 2 else near)[step // 2][...]
        panel[:, pl.ds(pl.multiple_of((own ^ step) * depth, depth), depth)] = held


def int_keep(screen_ref, ints_shape, pair_size):
    in_pair = lax.axis_index("grp") * ints_shape[0] // pair_size
    out_pair = lax.axis_index("pan") * ints_shape[1] // pair_size
    return screen_ref[in_pair, out_pair].astype(jnp.float32)


def product_blocks(panel, ints_ref):
    row_step = min(ROW_TILE, panel.shape[0])
    return [
        (row, column)
        for column in range(0, ints_ref.shape[1], COLUMN_TILE)
        for row in range(0, panel.shape[0], row_step)
    ]


def block_sums(panel, ints_ref, row, column):
    rows = slice(row, row + min(ROW_TILE, panel.shape[0]))
    ints = ints_ref[:, column : column + COLUMN_TILE]
    return jnp.dot(panel[rows, :], ints, preferred_element_type=jnp.float32)


def own_kernel(pair_size, near_count, part, int_screen_ref, *refs):
    near, other, refs = refs[:near_count], refs[near_count : 2 * near_count], refs[2 * near_count :]
    ints_ref, (sum_ref, panel) = refs[0], refs[-2:]
    keep = int_keep(int_screen_ref, ints_ref.shape, pair_size)
    depth, width = near[0].shape[1], panel.shape[1]
    own = lax.rem(lax.axis_index("pan"), ints_ref.shape[0] // depth)
    half = (own // (2 * near_count)) ^ part
    for at in range(2 * near_count):
        held = (other if at % 2 else near)[at // 2][...]
        column = lax.rem(own ^ at, 2 * near_count) * depth
        panel[:, pl.ds(pl.multiple_of(column, depth), depth)] = held
    depth_rows = pl.ds(pl.multiple_of(half * width, width), width)
    for row, column in product_blocks(panel, ints_ref):
        rows, columns = slice(row, row + min(ROW_TILE, panel.shape[0])), slice(column, column + COLUMN_TILE)
        sums = jnp.dot(panel[rows, :], ints_ref[depth_rows, columns], preferred_element_type=jnp.float32)
        if part:
            sums = sums + refs[1][rows, columns]
        sum_ref[rows, columns] = sums * keep if part else sums


def scale_of(digits, exponent):
    return digits * jnp.exp2(exponent) * (1.0 / (DIGITS * CODE_MAX))


def away_kernel(pair_size, near_count, first, int_screen_ref, *refs):
    near, refs = refs[:near_count], refs[near_count:]
    other, refs = (refs[0], refs[1:]) if refs[0].ndim == 3 else (refs[:near_count], refs[near_count:])
    other = [other.at[place] for place in range(near_count)] if not isinstance(other, (tuple, list)) else other
    ints_ref, before_ref = refs[:2]
    code_ref, scale_ref, panel = refs[-3:]
    keep = int_keep(int_screen_ref, ints_ref.shape, pair_size)
    lay_out(near, other, panel)
    scale_ref[...] = before_ref[...] if first else jnp.zeros_like(scale_ref)
    for row, column in product_blocks(panel, ints_ref):
        sums = block_sums(panel, ints_ref, row, column) * keep
        columns = slice(column, column + COLUMN_TILE)
        for at in range(0, sums.shape[0], TS):
            slot, rows = first + (row + at) // TS, slice(row + at, row + at + TS)
            part = sums[at : at + TS]
            top = jnp.maximum(jnp.max(jnp.abs(part), axis=0, keepdims=True), LEAST_SCALE)
            exponent = jnp.floor(jnp.log2(top))
            digits = jnp.ceil(top / jnp.exp2(exponent) * DIGITS)
            code = jnp.round(part * (1.0 / scale_of(digits, exponent)))
            code_ref[rows, columns] = code.astype(jnp.int32).astype(jnp.int16)
            scale_ref[slot : slot + 1, columns] = digits
            scale_ref[SCALE_ROWS + slot : SCALE_ROWS + slot + 1, columns] = exponent
    if first:
        code_ref[panel.shape[0] :, :] = scale_ref[...].astype(jnp.int32).astype(jnp.int16)


def product(kernel, int_screen, arrays, row_count, ints, out_rows_types, cost, name, parts=1):
    int_count, ab_count = ints.shape
    return pl.pallas_call(
        kernel,
        out_shape=[jax.ShapeDtypeStruct((rows, ab_count), dtype) for rows, dtype in out_rows_types],
        in_specs=[pl.BlockSpec(memory_space=pltpu.SMEM)]
        + [WHOLE] * len(arrays),
        out_specs=[WHOLE] * len(out_rows_types),
        scratch_shapes=[pltpu.VMEM((row_count, int_count // parts), ints.dtype)],
        compiler_params=pltpu.CompilerParams(vmem_limit_bytes=PRODUCT_VMEM),
        cost_estimate=cost,
        name=name,
    )(int_screen, *arrays)


def join_kernel(screen_ref, own_ref, *refs):
    code_refs, (out_hbm, held, sem) = refs[: len(SLOT_CHUNKS)], refs[len(SLOT_CHUNKS) :]
    grp_index = lax.axis_index("grp")
    first_tile = grp_index * BLOCK_TILES
    own_slots, own_count = live_slots(screen_ref, first_tile, grp_index)
    slots, count = live_slots(screen_ref, first_tile, 1 - grp_index)

    def tile_rows(slot):
        return pl.ds(pl.multiple_of(slot * TS, TS), TS)

    copies = []
    for part in range(own_ref.shape[1] // JOIN_TILE):
        columns = slice(part * JOIN_TILE, (part + 1) * JOIN_TILE)
        held_part = held.at[part]
        held_part[...] = jnp.zeros_like(held_part)
        last_ref = code_refs[-1]
        coded = last_ref[last_ref.shape[0] - 2 * SCALE_ROWS :, columns].astype(jnp.float32)
        scales = scale_of(coded[:SCALE_ROWS], coded[SCALE_ROWS:])
        for slot in range(LIVE_MAX):

            @pl.when(slot < own_count)
            def _():
                held_part[tile_rows(own_slots[slot]), :] = own_ref[slot * TS : (slot + 1) * TS, columns].astype(held.dtype)

        for (first, last), code_ref in zip(SLOT_CHUNKS, code_refs):
            for slot in range(first, last):

                @pl.when(slot < count)
                def _():
                    code = code_ref[(slot - first) * TS : (slot - first + 1) * TS, columns].astype(jnp.float32)
                    away = code * scales[slot : slot + 1]
                    at = jnp.int32(-1)
                    for own_slot in range(LIVE_MAX):
                        at = jnp.where((own_slot < own_count) & (own_slots[own_slot] == slots[slot]), own_slot, at)
                    own = own_ref[tile_rows(jnp.maximum(at, 0)), columns]
                    total = away + jnp.where(at >= 0, own, 0.0)
                    held_part[tile_rows(slots[slot]), :] = total.astype(held.dtype)

        copies.append(pltpu.make_async_copy(held_part, out_hbm.at[:, columns], sem.at[part]))
        copies[-1].start()
    for copy in copies:
        copy.wait()


def join(amp_screen, own_sum, codes, row_count):
    ab_count = own_sum.shape[1]
    arrays = [own_sum, *codes]
    return pl.pallas_call(
        join_kernel,
        out_shape=jax.ShapeDtypeStruct((row_count, ab_count), jnp.bfloat16),
        in_specs=[pl.BlockSpec(memory_space=pltpu.SMEM)] + [WHOLE] * len(arrays),
        out_specs=pl.BlockSpec(memory_space=pltpu.HBM),
        scratch_shapes=[
            pltpu.VMEM((ab_count // JOIN_TILE, row_count, JOIN_TILE), jnp.bfloat16),
            pltpu.SemaphoreType.DMA((ab_count // JOIN_TILE,)),
        ],
        compiler_params=pltpu.CompilerParams(vmem_limit_bytes=PRODUCT_VMEM),
        name="join",
    )(amp_screen, *arrays)


def routes(pan_count):
    half = pan_count // 2
    places = [(pan, grp) for pan in range(pan_count) for grp in range(2)]

    def at(pan, grp):
        return pan * 2 + grp

    def away(pan, grp):
        return pan // half != grp

    def flip(bits):
        return [(at(pan, grp), at(pan ^ bits, grp)) for pan, grp in places]

    first = [
        (at(pan, grp), at(pan, 1 - grp) if away(pan, grp) else at((pan + half) % pan_count, grp))
        for pan, grp in places
    ]
    across = [
        (at(pan, grp), at((pan + half) % pan_count, 1 - grp) if away(pan, grp) else at(pan ^ 1, grp))
        for pan, grp in places
    ]
    swap = [(at(pan, grp), at(pan, 1 - grp)) for pan, grp in places]
    return first, across, swap, flip


def near_blocks(block, flip, block_count):
    return [block] + [lax.ppermute(block, AXES, flip(bits)) for bits in range(2, block_count, 2)]


def two_group_shards(pan_count, amplitudes, integrals, amp_screen, int_screen):
    pair_size = TS * TS
    row_count, col_count = amplitudes.shape
    block_count = integrals.shape[0] // col_count
    if (
        row_count != BLOCK_TILES * TS
        or amp_screen.shape[1] != 2
        or integrals.shape[0] != pair_size
        or block_count * 2 != pan_count
    ):
        return shards(amplitudes, integrals, amp_screen, int_screen)
    first, across, swap, flip = routes(pan_count)
    is_own = lax.axis_index("pan") // (pan_count // 2) == lax.axis_index("grp")

    amp_screen = amp_screen.T
    picked = pick_live(amplitudes, amp_screen, pair_size)

    def crossed(near):
        return [lax.ppermute(block, AXES, flip(1)) for block in near]

    def away_product(near, other, before, first):
        rows = near[0].shape[0]
        code_rows = rows + (2 * SCALE_ROWS if first else 0)
        return product(
            functools.partial(away_kernel, pair_size, len(near), first), int_screen, [*near, *other, ints, before],
            rows, ints, ((code_rows, jnp.int16), (2 * SCALE_ROWS, jnp.float32)), LIGHT, "away_product",
        )

    def own_half(near, before, part):
        rows = own_block.shape[0]
        return product(
            functools.partial(own_kernel, pair_size, len(near), part), int_screen,
            [*near, *crossed(near), ints, *before], rows, ints, ((rows, jnp.float32),), MEDIUM, "own_product", 2,
        )[0]

    arrived = [(lax.ppermute(part, AXES, first), lax.ppermute(part, AXES, across)) for part in picked]
    own_block = jnp.concatenate([jnp.where(is_own, part, pair[0]) for part, pair in zip(picked, arrived)], axis=0)
    away_a, away_b = [jnp.where(is_own, *pair) for pair in arrived]
    ints, staged = stage(integrals, away_a)

    near_a = near_blocks(away_a, flip, block_count)
    near_a, staged = lax.optimization_barrier((near_a, staged))
    away_b, near_a = lax.optimization_barrier((away_b, near_a))
    other_a = [lax.ppermute(jnp.stack(near_a), AXES, flip(1))]
    code_a, scale_a = away_product(near_a, other_a, staged, 0)
    came_a = lax.ppermute(code_a, AXES, swap)
    near_b = near_blocks(away_b, flip, block_count)
    near_b, scale_a = lax.optimization_barrier((near_b, scale_a))
    own_block, near_b = lax.optimization_barrier((own_block, near_b))
    own_near = near_blocks(own_block, flip, block_count)
    code_b, _ = away_product(near_b, crossed(near_b), scale_a, SLOT_CHUNKS[1][0])
    came_b = lax.ppermute(code_b, AXES, swap)
    half = len(own_near) // 2
    near_low, near_high = own_near[:half], own_near[half:]
    own_sum = own_half(near_low, [], 0)
    near_high, came_a = lax.optimization_barrier((near_high, came_a))
    own_sum = own_half(near_high, [own_sum], 1)
    return join(amp_screen, own_sum, (came_a, came_b), row_count)


def column_pairs(piece_width, pair_size, pair_count):
    col_pair = jnp.arange(piece_width) // pair_size
    return (col_pair[None, :] == jnp.arange(pair_count)[:, None]).astype(jnp.bfloat16)


def shards(amplitudes, integrals, amp_screen, int_screen):
    pair_size = TS * TS
    row_count, col_count = amplitudes.shape
    int_count, ab_count = integrals.shape
    tile_count = row_count // TS
    pair_count = amp_screen.shape[1]
    grp_index = lax.axis_index("grp")
    pan_index = lax.axis_index("pan")
    screen_rows = lax.dynamic_slice_in_dim(amp_screen, grp_index * tile_count, tile_count, 0)
    in_pair = grp_index * int_count // pair_size
    out_pair = pan_index * ab_count // pair_size
    int_keep = int_screen[in_pair, out_pair].astype(jnp.bfloat16)
    int_panel = lax.all_gather(integrals * int_keep, "grp", axis=0, tiled=True)
    panel = lax.all_gather(amplitudes, "pan", axis=1, tiled=True)
    piece_width = panel.shape[1]
    onehot = column_pairs(piece_width, pair_size, pair_count)
    keep_mask = jnp.dot(
        screen_rows.astype(jnp.bfloat16), onehot, preferred_element_type=jnp.float32
    ).astype(jnp.bfloat16)
    masked = (panel.reshape(tile_count, TS, piece_width) * keep_mask[:, None, :]).reshape(
        row_count, piece_width
    )
    summed = jnp.dot(masked, int_panel, preferred_element_type=jnp.float32)
    return summed.astype(jnp.bfloat16)


def solution(mesh):
    in_specs = (P("grp", "pan"), P("grp", "pan"), P(), P())
    out_specs = P("grp", "pan")
    pan_count, grp_count = mesh.shape["pan"], mesh.shape["grp"]
    body = shards
    if grp_count == 2 and pan_count >= 4 and pan_count & (pan_count - 1) == 0:
        body = functools.partial(two_group_shards, pan_count)
    return jax.shard_map(body, mesh=mesh, in_specs=in_specs, out_specs=out_specs, check_vma=False)
```

```python
import functools

import jax
import jax.numpy as jnp
from jax import lax
from jax.experimental import pallas as pl
from jax.experimental.pallas import tpu as pltpu
from jax.sharding import PartitionSpec as P

TS = 64
LIVE_MAX = 4
BLOCK_TILES = 8
AXES = ("pan", "grp")
SLOT_CHUNKS = ((0, 2), (2, 4))
CODE_MAX = 32767.0
DIGITS = 8192.0
SCALE_ROWS = 8
STAGE_COPIES = 8
LEAST_SCALE = 1e-33
ROW_TILE = 128
COLUMN_TILE = 256
JOIN_TILE = 512
SMALL_VMEM = 8 * 1024 * 1024
PRODUCT_VMEM = 16 * 1024 * 1024
LIGHT = pl.CostEstimate(flops=1, bytes_accessed=1, transcendentals=0)
MEDIUM = pl.CostEstimate(flops=1 << 30, bytes_accessed=1, transcendentals=0)
WHOLE = pl.BlockSpec(memory_space=pltpu.VMEM)


def live_slots(screen_ref, first_tile, column):
    count = jnp.int32(0)
    slots = [jnp.int32(0)] * LIVE_MAX
    for tile in range(BLOCK_TILES):
        live = screen_ref[column, first_tile + tile] != 0
        for slot in range(LIVE_MAX):
            slots[slot] = jnp.where(live & (count == slot), tile, slots[slot])
        count = count + live.astype(jnp.int32)
    return slots, count


def pick_kernel(pair_size, screen_hbm, amps_hbm, *rest):
    picked_refs, (screen_ref, amps_ref, sem) = rest[:-3], rest[-3:]
    screen_copy = pltpu.make_async_copy(screen_hbm, screen_ref, sem.at[0])
    amps_copy = pltpu.make_async_copy(amps_hbm, amps_ref, sem.at[1])
    screen_copy.start()
    amps_copy.start()
    screen_copy.wait()
    column = lax.axis_index("pan") * amps_ref.shape[1] // pair_size
    slots, _ = live_slots(screen_ref, lax.axis_index("grp") * BLOCK_TILES, column)
    amps_copy.wait()
    for (first, last), picked_ref in zip(SLOT_CHUNKS, picked_refs):
        for slot in range(first, last):
            rows = pl.ds(pl.multiple_of(slots[slot] * TS, TS), TS)
            picked_ref[(slot - first) * TS : (slot - first + 1) * TS, :] = amps_ref[rows, :]


def pick_live(amplitudes, amp_screen, pair_size):
    return pl.pallas_call(
        functools.partial(pick_kernel, pair_size),
        out_shape=[
            jax.ShapeDtypeStruct(((last - first) * TS, amplitudes.shape[1]), amplitudes.dtype)
            for first, last in SLOT_CHUNKS
        ],
        in_specs=[pl.BlockSpec(memory_space=pltpu.HBM)] * 2,
        out_specs=[WHOLE] * len(SLOT_CHUNKS),
        scratch_shapes=[
            pltpu.SMEM(amp_screen.shape, amp_screen.dtype),
            pltpu.VMEM(amplitudes.shape, amplitudes.dtype),
            pltpu.SemaphoreType.DMA((2,)),
        ],
        compiler_params=pltpu.CompilerParams(vmem_limit_bytes=SMALL_VMEM),
        name="pick_live",
    )(in_hbm(amp_screen), in_hbm(amplitudes))


def in_hbm(array):
    return pltpu.with_memory_space_constraint(array, pltpu.HBM)


def stage_kernel(ints_hbm, after, ints_ref, staged_ref, sem):
    del after
    staged_ref[...] = jnp.zeros_like(staged_ref)
    rows = ints_hbm.shape[0] // STAGE_COPIES
    copies = [
        pltpu.make_async_copy(
            ints_hbm.at[pl.ds(part * rows, rows), :], ints_ref.at[pl.ds(part * rows, rows), :], sem.at[part]
        )
        for part in range(STAGE_COPIES)
    ]
    for copy in copies:
        copy.start()
    for copy in copies:
        copy.wait()


def stage(integrals, after):
    return pl.pallas_call(
        stage_kernel,
        out_shape=[pltpu.VMEM(integrals.shape, integrals.dtype), jax.ShapeDtypeStruct((8, 128), jnp.float32)],
        in_specs=[pl.BlockSpec(memory_space=pltpu.HBM), pl.BlockSpec(memory_space=pl.ANY)],
        out_specs=[WHOLE] * 2,
        scratch_shapes=[pltpu.SemaphoreType.DMA((STAGE_COPIES,))],
        compiler_params=pltpu.CompilerParams(vmem_limit_bytes=SMALL_VMEM),
        cost_estimate=LIGHT,
        name="stage_integrals",
    )(in_hbm(integrals), after)


def lay_out(near, other, panel):
    depth = near[0].shape[1]
    own = lax.rem(lax.axis_index("pan"), 2 * len(near))
    for step in range(2 * len(near)):
        held = (other if step % 2 else near)[step // 2][...]
        panel[:, pl.ds(pl.multiple_of((own ^ step) * depth, depth), depth)] = held


def int_keep(screen_ref, ints_shape, pair_size):
    in_pair = lax.axis_index("grp") * ints_shape[0] // pair_size
    out_pair = lax.axis_index("pan") * ints_shape[1] // pair_size
    return screen_ref[in_pair, out_pair].astype(jnp.float32)


def product_blocks(panel, ints_ref):
    row_step = min(ROW_TILE, panel.shape[0])
    return [
        (row, column)
        for column in range(0, ints_ref.shape[1], COLUMN_TILE)
        for row in range(0, panel.shape[0], row_step)
    ]


def block_sums(panel, ints_ref, row, column):
    rows = slice(row, row + min(ROW_TILE, panel.shape[0]))
    ints = ints_ref[:, column : column + COLUMN_TILE]
    return jnp.dot(panel[rows, :], ints, preferred_element_type=jnp.float32)


def own_kernel(pair_size, near_count, part, int_screen_ref, *refs):
    near, other, refs = refs[:near_count], refs[near_count : 2 * near_count], refs[2 * near_count :]
    ints_ref, (sum_ref, panel) = refs[0], refs[-2:]
    keep = int_keep(int_screen_ref, ints_ref.shape, pair_size)
    depth, width = near[0].shape[1], panel.shape[1]
    own = lax.rem(lax.axis_index("pan"), ints_ref.shape[0] // depth)
    half = (own // (2 * near_count)) ^ part
    for at in range(2 * near_count):
        held = (other if at % 2 else near)[at // 2][...]
        column = lax.rem(own ^ at, 2 * near_count) * depth
        panel[:, pl.ds(pl.multiple_of(column, depth), depth)] = held
    depth_rows = pl.ds(pl.multiple_of(half * width, width), width)
    for row, column in product_blocks(panel, ints_ref):
        rows, columns = slice(row, row + min(ROW_TILE, panel.shape[0])), slice(column, column + COLUMN_TILE)
        sums = jnp.dot(panel[rows, :], ints_ref[depth_rows, columns], preferred_element_type=jnp.float32)
        if part:
            sums = sums + refs[1][rows, columns]
        sum_ref[rows, columns] = sums * keep if part else sums


def scale_of(digits, exponent):
    return digits * jnp.exp2(exponent) * (1.0 / (DIGITS * CODE_MAX))


def away_kernel(pair_size, near_count, first, int_screen_ref, *refs):
    near, refs = refs[:near_count], refs[near_count:]
    other, refs = (refs[0], refs[1:]) if refs[0].ndim == 3 else (refs[:near_count], refs[near_count:])
    other = [other.at[place] for place in range(near_count)] if not isinstance(other, (tuple, list)) else other
    ints_ref, before_ref = refs[:2]
    code_ref, scale_ref, panel = refs[-3:]
    keep = int_keep(int_screen_ref, ints_ref.shape, pair_size)
    lay_out(near, other, panel)
    scale_ref[...] = before_ref[...] if first else jnp.zeros_like(scale_ref)
    for row, column in product_blocks(panel, ints_ref):
        sums = block_sums(panel, ints_ref, row, column) * keep
        columns = slice(column, column + COLUMN_TILE)
        for at in range(0, sums.shape[0], TS):
            slot, rows = first + (row + at) // TS, slice(row + at, row + at + TS)
            part = sums[at : at + TS]
            top = jnp.maximum(jnp.max(jnp.abs(part), axis=0, keepdims=True), LEAST_SCALE)
            exponent = jnp.floor(jnp.log2(top))
            digits = jnp.ceil(top / jnp.exp2(exponent) * DIGITS)
            code = jnp.round(part * (1.0 / scale_of(digits, exponent)))
            code_ref[rows, columns] = code.astype(jnp.int32).astype(jnp.int16)
            scale_ref[slot : slot + 1, columns] = digits
            scale_ref[SCALE_ROWS + slot : SCALE_ROWS + slot + 1, columns] = exponent
    if first:
        code_ref[panel.shape[0] :, :] = scale_ref[...].astype(jnp.int32).astype(jnp.int16)


def product(kernel, int_screen, arrays, gates, row_count, ints, out_rows_types, cost, name, parts=1):
    int_count, ab_count = ints.shape
    return pl.pallas_call(
        kernel,
        out_shape=[jax.ShapeDtypeStruct((rows, ab_count), dtype) for rows, dtype in out_rows_types],
        in_specs=[pl.BlockSpec(memory_space=pltpu.SMEM)]
        + [WHOLE] * len(arrays)
        + [pl.BlockSpec(memory_space=pl.ANY)] * len(gates),
        out_specs=[WHOLE] * len(out_rows_types),
        scratch_shapes=[pltpu.VMEM((row_count, int_count // parts), ints.dtype)],
        compiler_params=pltpu.CompilerParams(vmem_limit_bytes=PRODUCT_VMEM),
        cost_estimate=cost,
        name=name,
    )(int_screen, *arrays, *gates)


def join_kernel(screen_ref, own_ref, *refs):
    code_refs, (out_hbm, held, sem) = refs[: len(SLOT_CHUNKS)], refs[len(SLOT_CHUNKS) :]
    grp_index = lax.axis_index("grp")
    first_tile = grp_index * BLOCK_TILES
    own_slots, own_count = live_slots(screen_ref, first_tile, grp_index)
    slots, count = live_slots(screen_ref, first_tile, 1 - grp_index)

    def tile_rows(slot):
        return pl.ds(pl.multiple_of(slot * TS, TS), TS)

    copies = []
    for part in range(own_ref.shape[1] // JOIN_TILE):
        columns = slice(part * JOIN_TILE, (part + 1) * JOIN_TILE)
        held_part = held.at[part]
        held_part[...] = jnp.zeros_like(held_part)
        last_ref = code_refs[-1]
        coded = last_ref[last_ref.shape[0] - 2 * SCALE_ROWS :, columns].astype(jnp.float32)
        scales = scale_of(coded[:SCALE_ROWS], coded[SCALE_ROWS:])
        for slot in range(LIVE_MAX):

            @pl.when(slot < own_count)
            def _():
                held_part[tile_rows(own_slots[slot]), :] = own_ref[slot * TS : (slot + 1) * TS, columns].astype(held.dtype)

        for (first, last), code_ref in zip(SLOT_CHUNKS, code_refs):
            for slot in range(first, last):

                @pl.when(slot < count)
                def _():
                    code = code_ref[(slot - first) * TS : (slot - first + 1) * TS, columns].astype(jnp.float32)
                    away = code * scales[slot : slot + 1]
                    at = jnp.int32(-1)
                    for own_slot in range(LIVE_MAX):
                        at = jnp.where((own_slot < own_count) & (own_slots[own_slot] == slots[slot]), own_slot, at)
                    own = own_ref[tile_rows(jnp.maximum(at, 0)), columns]
                    total = away + jnp.where(at >= 0, own, 0.0)
                    held_part[tile_rows(slots[slot]), :] = total.astype(held.dtype)

        copies.append(pltpu.make_async_copy(held_part, out_hbm.at[:, columns], sem.at[part]))
        copies[-1].start()
    for copy in copies:
        copy.wait()


def join(amp_screen, own_sum, codes, row_count):
    ab_count = own_sum.shape[1]
    arrays = [own_sum, *codes]
    return pl.pallas_call(
        join_kernel,
        out_shape=jax.ShapeDtypeStruct((row_count, ab_count), jnp.bfloat16),
        in_specs=[pl.BlockSpec(memory_space=pltpu.SMEM)] + [WHOLE] * len(arrays),
        out_specs=pl.BlockSpec(memory_space=pltpu.HBM),
        scratch_shapes=[
            pltpu.VMEM((ab_count // JOIN_TILE, row_count, JOIN_TILE), jnp.bfloat16),
            pltpu.SemaphoreType.DMA((ab_count // JOIN_TILE,)),
        ],
        compiler_params=pltpu.CompilerParams(vmem_limit_bytes=PRODUCT_VMEM),
        name="join",
    )(amp_screen, *arrays)


def routes(pan_count):
    half = pan_count // 2
    places = [(pan, grp) for pan in range(pan_count) for grp in range(2)]

    def at(pan, grp):
        return pan * 2 + grp

    def away(pan, grp):
        return pan // half != grp

    def flip(bits):
        return [(at(pan, grp), at(pan ^ bits, grp)) for pan, grp in places]

    first = [
        (at(pan, grp), at(pan, 1 - grp) if away(pan, grp) else at((pan + half) % pan_count, grp))
        for pan, grp in places
    ]
    across = [
        (at(pan, grp), at((pan + half) % pan_count, 1 - grp) if away(pan, grp) else at(pan ^ 1, grp))
        for pan, grp in places
    ]
    swap = [(at(pan, grp), at(pan, 1 - grp)) for pan, grp in places]
    return first, across, swap, flip


def near_blocks(block, flip, block_count):
    return [block] + [lax.ppermute(block, AXES, flip(bits)) for bits in range(2, block_count, 2)]


def two_group_shards(pan_count, amplitudes, integrals, amp_screen, int_screen):
    pair_size = TS * TS
    row_count, col_count = amplitudes.shape
    block_count = integrals.shape[0] // col_count
    if (
        row_count != BLOCK_TILES * TS
        or amp_screen.shape[1] != 2
        or integrals.shape[0] != pair_size
        or block_count * 2 != pan_count
    ):
        return shards(amplitudes, integrals, amp_screen, int_screen)
    first, across, swap, flip = routes(pan_count)
    is_own = lax.axis_index("pan") // (pan_count // 2) == lax.axis_index("grp")

    amp_screen = amp_screen.T
    picked = pick_live(amplitudes, amp_screen, pair_size)

    def crossed(near):
        return [lax.ppermute(block, AXES, flip(1)) for block in near]

    def away_product(near, other, before, first):
        rows = near[0].shape[0]
        code_rows = rows + (2 * SCALE_ROWS if first else 0)
        return product(
            functools.partial(away_kernel, pair_size, len(near), first), int_screen, [*near, *other, ints, before], [],
            rows, ints, ((code_rows, jnp.int16), (2 * SCALE_ROWS, jnp.float32)), LIGHT, "away_product",
        )

    def own_half(near, before, part):
        rows = own_block.shape[0]
        return product(
            functools.partial(own_kernel, pair_size, len(near), part), int_screen,
            [*near, *crossed(near), ints, *before], [gate], rows, ints, ((rows, jnp.float32),), MEDIUM, "own_product", 2,
        )[0]

    arrived = [(lax.ppermute(part, AXES, first), lax.ppermute(part, AXES, across)) for part in picked]
    own_block = jnp.concatenate([jnp.where(is_own, part, pair[0]) for part, pair in zip(picked, arrived)], axis=0)
    away_a, away_b = [jnp.where(is_own, *pair) for pair in arrived]
    ints, staged = stage(integrals, away_a)

    near_a = near_blocks(away_a, flip, block_count)
    near_a, staged = lax.optimization_barrier((near_a, staged))
    away_b, near_a = lax.optimization_barrier((away_b, near_a))
    other_a = [lax.ppermute(jnp.stack(near_a), AXES, flip(1))]
    code_a, scale_a = away_product(near_a, other_a, staged, 0)
    came_a = lax.ppermute(code_a, AXES, swap)
    near_b = near_blocks(away_b, flip, block_count)
    near_b, scale_a = lax.optimization_barrier((near_b, scale_a))
    own_block, gate = lax.optimization_barrier((own_block, scale_a))
    own_near = near_blocks(own_block, flip, block_count)
    code_b, _ = away_product(near_b, crossed(near_b), scale_a, SLOT_CHUNKS[1][0])
    came_b = lax.ppermute(code_b, AXES, swap)
    half = len(own_near) // 2
    near_low, near_high = own_near[:half], own_near[half:]
    own_sum = own_half(near_low, [], 0)
    near_high, came_a = lax.optimization_barrier((near_high, came_a))
    own_sum = own_half(near_high, [own_sum], 1)
    return join(amp_screen, own_sum, (came_a, came_b), row_count)


def column_pairs(piece_width, pair_size, pair_count):
    col_pair = jnp.arange(piece_width) // pair_size
    return (col_pair[None, :] == jnp.arange(pair_count)[:, None]).astype(jnp.bfloat16)


def shards(amplitudes, integrals, amp_screen, int_screen):
    pair_size = TS * TS
    row_count, col_count = amplitudes.shape
    int_count, ab_count = integrals.shape
    tile_count = row_count // TS
    pair_count = amp_screen.shape[1]
    grp_index = lax.axis_index("grp")
    pan_index = lax.axis_index("pan")
    screen_rows = lax.dynamic_slice_in_dim(amp_screen, grp_index * tile_count, tile_count, 0)
    in_pair = grp_index * int_count // pair_size
    out_pair = pan_index * ab_count // pair_size
    int_keep = int_screen[in_pair, out_pair].astype(jnp.bfloat16)
    int_panel = lax.all_gather(integrals * int_keep, "grp", axis=0, tiled=True)
    panel = lax.all_gather(amplitudes, "pan", axis=1, tiled=True)
    piece_width = panel.shape[1]
    onehot = column_pairs(piece_width, pair_size, pair_count)
    keep_mask = jnp.dot(
        screen_rows.astype(jnp.bfloat16), onehot, preferred_element_type=jnp.float32
    ).astype(jnp.bfloat16)
    masked = (panel.reshape(tile_count, TS, piece_width) * keep_mask[:, None, :]).reshape(
        row_count, piece_width
    )
    summed = jnp.dot(masked, int_panel, preferred_element_type=jnp.float32)
    return summed.astype(jnp.bfloat16)


def solution(mesh):
    in_specs = (P("grp", "pan"), P("grp", "pan"), P(), P())
    out_specs = P("grp", "pan")
    pan_count, grp_count = mesh.shape["pan"], mesh.shape["grp"]
    body = shards
    if grp_count == 2 and pan_count >= 4 and pan_count & (pan_count - 1) == 0:
        body = functools.partial(two_group_shards, pan_count)
    return jax.shard_map(body, mesh=mesh, in_specs=in_specs, out_specs=out_specs, check_vma=False)
```
